512 devices in a mesh: chan: 8 (over x, y_hi), tm: 64 (over z, y_lo, core).
Axes of the slice: x: 4, y: 4 (y_hi: 2, y_lo: 2; y = y_hi * 2 + y_lo), z: 16, core: 2. Of those that a mesh axis runs over, the one named last changes fastest.
Arguments:
- launched: float32 [2, 96, 2, 524288], P(None, 'chan', None, 'tm'), may hold values from -6 to 6
- amp_noise: bfloat16 [2, 96, 2, 524288], P(None, 'chan', None, 'tm'), may hold values from -4 to 4
- window_start: int32 [96, 96], replicated, may hold values from -512 to 384, as said below
- window_length: int32 [96, 96], replicated, may hold values from 128 to 1024, as said below
Outputs:
- received: float32 [2, 96, 2, 524288], P(None, 'chan', None, 'tm')
The draws below stay inside these ranges and needn't reach their ends.
Inputs may be any that keep to these rules, and one draw needn't show every extreme that they name: window_start: a multiple of 128; window_start + window_length <= 512 for every pair; for every channel c the pair (c, (c + 1) mod 96) has start -512. window_length: a multiple of 128; for every channel c the pair (c, (c + 1) mod 96) has length 1024.
All inputs are finite; a program needn't handle non-finite values.
Results may differ from the reference program's by a relative error of at most 0.0003.
Values sent between devices are 32-bit elements; how exact they have to be, the bound alone decides.
No kernel may reach another device: no remote copies, remote signals or barrier semaphores. Data moves between devices by JAX's collectives and lax.ppermute only.
A program may use at most 64 MiB of HBM per device.

```python
import jax
import jax.numpy as jnp
from jax import lax

HALO = 512
CHANNELS = 96
SAMPLES = 524288


def window_blocks(key):
    block_count = 2 * HALO // 128
    start_key = jax.random.fold_in(key, 11)
    length_key = jax.random.fold_in(key, 12)
    first_block = jax.random.randint(start_key, (CHANNELS, CHANNELS), 0, block_count)
    extent = 1 + jax.random.randint(length_key, (CHANNELS, CHANNELS), 0, block_count - first_block)
    rows_idx = lax.broadcasted_iota(jnp.int32, (CHANNELS, CHANNELS), 0)
    cols_idx = lax.broadcasted_iota(jnp.int32, (CHANNELS, CHANNELS), 1)
    widest = cols_idx == (rows_idx + 1) % CHANNELS
    first_block = jnp.where(widest, 0, first_block)
    extent = jnp.where(widest, block_count, extent)
    return (first_block, extent)


def draw_window_start(key, part):
    first_block, extent = window_blocks(key)
    return (first_block * 128 - HALO).astype(jnp.int32)


def draw_window_length(key, part):
    first_block, extent = window_blocks(key)
    return (extent * 128).astype(jnp.int32)


def level_of(own_key, shape, pieces, low, top_value):
    factor_of, own = 1.0, jax.random.fold_in(own_key, 6)
    for dim, parts in pieces:
        heights = jnp.exp(jax.random.uniform(jax.random.fold_in(own, dim), (parts,), jnp.float32, low / len(pieces), top_value / len(pieces)))
        factor_of = factor_of * jnp.repeat(heights, shape[dim] // parts).reshape([-1 if axis == dim else 1 for axis in range(len(shape))])
    return factor_of


def gaussian(rng, shape, deviation, most, shards=(), held_as=jnp.bfloat16):
    gain = level_of(rng, shape, shards, -0.22, 0.18) if shards else 1.0
    drawn = jax.random.normal(rng, shape, jnp.float32) * deviation * gain
    return jnp.minimum(jnp.maximum(drawn, -most), most).astype(held_as)


def setup_inputs(seed: int = 0) -> dict:
    splits = jax.random.split(jax.random.key(seed), 5)
    return {
        "launched": gaussian(splits[0], (2, CHANNELS, 2, SAMPLES), 1.0, 6.0, ((1, 8), (3, 64)), jnp.float32),
        "amp_noise": gaussian(splits[1], (2, CHANNELS, 2, SAMPLES), 0.3, 4.0, ((1, 8), (3, 64))),
        "window_start": draw_window_start(jax.random.fold_in(splits[4], 71), 0),
        "window_length": draw_window_length(jax.random.fold_in(splits[4], 71), 0),
    }


gamma_self = 0.1
gamma_cross = 0.05
highest = lax.Precision.HIGHEST


def square_residue(signed_ids, modulus):
    base_value = signed_ids % modulus
    running = jnp.zeros_like(base_value)
    for shift_bits in (16, 8, 0):
        digit = (base_value // (1 << shift_bits)) % 256
        running = (running * 256) % modulus
        running = (running + base_value * digit) % modulus
    return running


def window_weights(starts, lengths, target_ids, source_ids, float_type):
    shift_count = 2 * HALO // 128
    offsets = (lax.iota(jnp.int32, shift_count) * 128 - HALO)[:, None, None]
    inside = (starts[None] <= offsets) & (offsets + 128 <= starts[None] + lengths[None])
    others = (target_ids[:, None] != source_ids[None, :])[None]
    inverse = 1.0 / lengths[None].astype(float_type)
    return jnp.where(inside & others, inverse, jnp.zeros_like(inverse))


def slide_tables(float_type):
    rows_idx = lax.broadcasted_iota(jnp.int32, (128, 128), 0)
    cols_idx = lax.broadcasted_iota(jnp.int32, (128, 128), 1)
    return (rows_idx >= cols_idx).astype(float_type), (rows_idx < cols_idx).astype(float_type)


def reference(launched, amp_noise, window_start, window_length):
    float_type = launched.dtype
    channels = launched.shape[1]
    samples = launched.shape[3]
    optical = lax.complex(launched[0], launched[1])
    spectrum = jnp.fft.fft(optical, axis=-1)
    freq_ids = lax.iota(jnp.int32, samples)
    signed_ids = jnp.where(freq_ids < samples // 2, freq_ids, freq_ids - samples)
    modulus = 4 * samples
    residue = square_residue(signed_ids, modulus)
    angles = residue.astype(float_type) * (2.0 * jnp.pi / modulus)
    spectrum = spectrum * lax.complex(jnp.cos(angles), jnp.sin(angles))
    optical = jnp.fft.ifft(spectrum, axis=-1)
    real_part = jnp.real(optical)
    imag_part = jnp.imag(optical)
    powers = jnp.sum(real_part * real_part + imag_part * imag_part, axis=1)
    blocks = powers.reshape(channels, samples // 128, 128)
    following = jnp.roll(blocks, -1, axis=1)
    upper_tri, lower_tri = slide_tables(float_type)
    sliding = jnp.einsum("cnq,qr->cnr", blocks, upper_tri, precision=highest)
    sliding = sliding + jnp.einsum("cnq,qr->cnr", following, lower_tri, precision=highest)
    sliding = sliding.reshape(channels, samples)
    chan_ids = lax.iota(jnp.int32, channels)
    weights_all = window_weights(window_start, window_length, chan_ids, chan_ids, float_type)
    cross_sum = jnp.zeros((channels, samples), float_type)
    for offset_idx in range(2 * HALO // 128):
        shifted = jnp.roll(sliding, HALO - 128 * offset_idx, axis=1)
        cross_sum = cross_sum + jnp.dot(weights_all[offset_idx], shifted, precision=highest, preferred_element_type=jnp.float32)
    phases = (gamma_self * powers + gamma_cross * cross_sum)[:, None, :]
    noise_full = amp_noise.astype(float_type)
    out_real = jnp.cos(phases) * real_part - jnp.sin(phases) * imag_part + noise_full[0]
    out_imag = jnp.cos(phases) * imag_part + jnp.sin(phases) * real_part + noise_full[1]
    return jnp.stack([out_real, out_imag])
```

```python
import functools

import jax
import jax.numpy as jnp
import ml_dtypes
import numpy as np
from jax import lax
from jax.experimental import pallas as pl
from jax.experimental.pallas import tpu as pltpu
from jax.sharding import Mesh
from jax.sharding import PartitionSpec as P

HALO = 512
GAMMA_SELF = 0.1
GAMMA_CROSS = 0.05
SAMPLES = 524288
LANES = 128
COARSE = 8
FOLDED = SAMPLES // COARSE
OUTER = FOLDED // LANES
highest = lax.Precision.HIGHEST


def split_np(matrix):
    upper = matrix.astype(ml_dtypes.bfloat16)
    lower = (matrix - upper.astype(np.float64)).astype(ml_dtypes.bfloat16)
    return np.stack([upper, lower])


def roots(numerators, period):
    angles = (numerators % period) * (2.0 * np.pi / period)
    return np.cos(angles), np.sin(angles)


@functools.cache
def tables():
    outer_ids = np.arange(OUTER, dtype=np.int64)
    lane_ids = np.arange(LANES, dtype=np.int64)
    residues = np.arange(COARSE, dtype=np.int64)
    cosine, sine = roots(outer_ids[:, None] * outer_ids[None, :], OUTER)
    outer = np.stack([split_np(cosine), split_np(sine)])
    cosine, sine = roots(lane_ids[:, None] * lane_ids[None, :], LANES)
    forward = np.block([[cosine, -sine], [sine, cosine]])
    inner = np.stack([split_np(forward), split_np(forward.T)])
    turn = np.stack(roots(outer_ids[:, None] * lane_ids[None, :], FOLDED)).astype(np.float32)
    time_ids = LANES * outer_ids[:, None] + lane_ids[None, :]
    shift = np.stack(roots(residues[:, None, None] * time_ids[None], SAMPLES), axis=1)
    freq_ids = residues[:, None, None] + COARSE * (
        outer_ids[None, :, None] + OUTER * lane_ids[None, None, :]
    )
    signed_ids = np.where(freq_ids < SAMPLES // 2, freq_ids, freq_ids - SAMPLES)
    response = np.stack(roots(signed_ids * signed_ids, 4 * SAMPLES), axis=1) / SAMPLES
    return outer, inner, turn, shift.astype(np.float32), response.astype(np.float32)


def radix_eight(parts, sign):
    half = np.float32(np.sqrt(0.5))

    def add(a, b):
        return a[0] + b[0], a[1] + b[1]

    def sub(a, b):
        return a[0] - b[0], a[1] - b[1]

    def quarter(a):
        return (-sign * a[1], sign * a[0])

    def eighth(a):
        return (half * (a[0] - sign * a[1]), half * (a[1] + sign * a[0]))

    def four(a, b, c, d):
        even_sum, even_diff = add(a, c), sub(a, c)
        odd_sum, odd_diff = add(b, d), quarter(sub(b, d))
        return (
            add(even_sum, odd_sum),
            add(even_diff, odd_diff),
            sub(even_sum, odd_sum),
            sub(even_diff, odd_diff),
        )

    even = four(*(add(parts[i], parts[i + 4]) for i in range(4)))
    diffs = [sub(parts[i], parts[i + 4]) for i in range(4)]
    odd = four(
        diffs[0], eighth(diffs[1]), quarter(diffs[2]), quarter(eighth(diffs[3]))
    )
    return [pair for both in zip(even, odd) for pair in both]


def fold_kernel(sign, in_ref, out_ref):
    rows = 8

    @pl.loop(0, in_ref.shape[3] // rows)
    def _(step):
        at = pl.ds(pl.multiple_of(step * rows, rows), rows)
        parts = [(in_ref[i, 0, 0, at, :], in_ref[i, 1, 0, at, :]) for i in range(COARSE)]
        for i, pair in enumerate(radix_eight(parts, sign)):
            out_ref[i, 0, 0, at, :] = pair[0]
            out_ref[i, 1, 0, at, :] = pair[1]


def fold(values, sign):
    spec = pl.BlockSpec((8, 2, 1, 64, 128), lambda row: (0, 0, row, 0, 0))
    return pl.pallas_call(
        functools.partial(fold_kernel, sign),
        grid=(values.shape[2],),
        in_specs=[spec],
        out_specs=spec,
        out_shape=jax.ShapeDtypeStruct(values.shape, jnp.float32),
    )(values)


def halves(values):
    upper = values.astype(jnp.bfloat16)
    lower = (values - upper.astype(jnp.float32)).astype(jnp.bfloat16)
    return upper, lower


def dot(left, right):
    return jnp.dot(left, right, preferred_element_type=jnp.float32)


def triple(left, right):
    return dot(left[0], right[0]) + (dot(left[0], right[1]) + dot(left[1], right[0]))


def disperse_kernel(
    residue_ref, in_ref, outer_ref, inner_ref, turn_ref, shift_ref, response_ref, out_ref
):
    def turned(real, imag, cosine, sine, sign):
        if sign > 0:
            return real * cosine - imag * sine, imag * cosine + real * sine
        return real * cosine + imag * sine, imag * cosine - real * sine

    def packed(real, imag):
        return halves(jnp.concatenate([real, imag], axis=1))

    cosines = (outer_ref[0, 0], outer_ref[0, 1])
    sines = (outer_ref[1, 0], outer_ref[1, 1])
    shift = (shift_ref[0, 0], shift_ref[0, 1])
    turn = (turn_ref[0], turn_ref[1])
    real = in_ref[:, 0, 0].reshape(OUTER, LANES)
    imag = in_ref[:, 1, 0].reshape(OUTER, LANES)
    values = packed(*turned(real, imag, *shift, -1))
    by_cos, by_sin = triple(cosines, values), triple(sines, values)
    real = by_cos[:, :LANES] + by_sin[:, LANES:]
    imag = by_cos[:, LANES:] - by_sin[:, :LANES]
    values = packed(*turned(real, imag, *turn, -1))
    both = triple(values, (inner_ref[0, 0], inner_ref[0, 1]))
    real, imag = turned(
        both[:, :LANES], both[:, LANES:], response_ref[0, 0], response_ref[0, 1], 1
    )
    both = triple(packed(real, imag), (inner_ref[1, 0], inner_ref[1, 1]))
    values = packed(*turned(both[:, :LANES], both[:, LANES:], *turn, 1))
    by_cos, by_sin = triple(cosines, values), triple(sines, values)
    real = by_cos[:, :LANES] - by_sin[:, LANES:]
    imag = by_cos[:, LANES:] + by_sin[:, :LANES]
    real, imag = turned(real, imag, *shift, 1)
    out_ref[:, 0, 0] = real.reshape(8, 64, LANES)
    out_ref[:, 1, 0] = imag.reshape(8, 64, LANES)


def disperse(values, residue):
    spec = pl.BlockSpec((8, 2, 1, 64, 128), lambda row, res: (0, 0, row, 0, 0))
    outer, inner, turn, shift, response = tables()

    def whole(table):
        return pl.BlockSpec(table.shape, lambda row, res: (0,) * table.ndim)

    def one_residue(table):
        return pl.BlockSpec((1,) + table.shape[1:], lambda row, res: (res[0], 0, 0, 0))

    return pl.pallas_call(
        disperse_kernel,
        grid_spec=pltpu.PrefetchScalarGridSpec(
            num_scalar_prefetch=1,
            grid=(values.shape[2],),
            in_specs=[
                spec,
                whole(outer),
                whole(inner),
                whole(turn),
                one_residue(shift),
                one_residue(response),
            ],
            out_specs=spec,
        ),
        out_shape=jax.ShapeDtypeStruct(values.shape, jnp.float32),
        compiler_params=pltpu.CompilerParams(vmem_limit_bytes=40 * 1024 * 1024),
    )(residue, values, outer, inner, turn, shift, response)


def window_weights(starts, lengths):
    channels = starts.shape[0]
    shift_count = 2 * HALO // 128
    offsets = (lax.iota(jnp.int32, shift_count) * 128 - HALO)[None, :, None]
    starts, lengths = starts[:, None, :], lengths[:, None, :]
    inside = (starts <= offsets) & (offsets + 128 <= starts + lengths)
    ids = lax.iota(jnp.int32, channels)
    others = (ids[:, None] != ids[None, :])[:, None, :]
    inverse = 1.0 / lengths.astype(jnp.float32)
    weights = jnp.where(inside & others, inverse, jnp.zeros_like(inverse))
    return weights.reshape(channels, shift_count * channels)


def cross_kernel(weights_ref, in_ref, out_ref):
    weights = halves(weights_ref[...])
    channels, depth = weights_ref.shape
    for step in range(out_ref.shape[1]):
        values = halves(in_ref[step * channels : step * channels + depth, :])
        out_ref[:, step, :] = triple(weights, values)


def slide_tables():
    rows_idx = lax.broadcasted_iota(jnp.int32, (128, 128), 0)
    cols_idx = lax.broadcasted_iota(jnp.int32, (128, 128), 1)
    return ((rows_idx >= cols_idx).astype(jnp.float32), (rows_idx < cols_idx).astype(jnp.float32))


def exchange(values, axis):
    return lax.all_to_all(values, axis, 0, 0, tiled=True)


def per_device(launched, amp_noise, window_start, window_length):
    channels = window_start.shape[0]
    local_chan = launched.shape[1]
    rows = 2 * local_chan
    blocks = launched.shape[3] // LANES
    residue = lax.axis_index("i").astype(jnp.int32).reshape(1)
    values = launched.reshape(2, COARSE, rows // COARSE, blocks, LANES).transpose(1, 0, 2, 3, 4)
    values = exchange(values, "j")
    values = fold(values, -1)
    values = exchange(values, "i")
    values = disperse(values, residue)
    values = exchange(values, "i")
    values = fold(values, 1)
    values = exchange(values, "j")
    fields = values.transpose(1, 0, 2, 3, 4).reshape(2, local_chan, 2, blocks, LANES)
    powers = jnp.sum(fields * fields, axis=(0, 2))
    count = lax.axis_size("j") * lax.axis_size("i")
    up = [(k, (k + 1) % count) for k in range(count)]
    down = [(k, j) for j, k in up]
    reach = HALO // LANES
    before = lax.ppermute(powers[:, blocks - reach :], ("j", "i"), up)
    after = lax.ppermute(powers[:, :reach], ("j", "i"), down)
    extended = jnp.concatenate([before, powers, after], axis=1)
    upper_tri, lower_tri = slide_tables()
    sliding = jnp.einsum("cnq,qr->cnr", extended[:, :-1], upper_tri, precision=highest)
    sliding = sliding + jnp.einsum("cnq,qr->cnr", extended[:, 1:], lower_tri, precision=highest)
    groups = lax.axis_size("chan")
    own = blocks // groups
    taken = own + 2 * reach - 1
    pieces = jnp.stack([sliding[:, own * k : own * k + taken] for k in range(groups)])
    pieces = exchange(pieces, "chan")
    pieces = pieces.transpose(2, 0, 1, 3).reshape(taken * channels, LANES)
    weights = window_weights(window_start, window_length)
    cross = pl.pallas_call(
        cross_kernel,
        out_shape=jax.ShapeDtypeStruct((channels, own, LANES), jnp.float32),
    )(weights, pieces)
    cross = exchange(cross.reshape(groups, local_chan, own, LANES), "chan")
    cross = cross.transpose(1, 0, 2, 3).reshape(local_chan, blocks, LANES)
    phases = (GAMMA_SELF * powers + GAMMA_CROSS * cross)[:, None]
    cosine, sine = jnp.cos(phases), jnp.sin(phases)
    out_real = cosine * fields[0] - sine * fields[1]
    out_imag = cosine * fields[1] + sine * fields[0]
    received = jnp.stack([out_real, out_imag]).reshape(launched.shape)
    return received + amp_noise.astype(jnp.float32)


def solution(mesh):
    split = Mesh(mesh.devices.reshape(mesh.shape["chan"], COARSE, -1), ("chan", "j", "i"))
    fields = P(None, "chan", None, ("j", "i"))
    return jax.shard_map(
        per_device,
        mesh=split,
        in_specs=(fields, fields, P(), P()),
        out_specs=fields,
        check_vma=False,
    )
```

```python
import functools

import jax
import jax.numpy as jnp
import ml_dtypes
import numpy as np
from jax import lax
from jax.experimental import pallas as pl
from jax.experimental.pallas import tpu as pltpu
from jax.sharding import Mesh
from jax.sharding import PartitionSpec as P

HALO = 512
GAMMA_SELF = 0.1
GAMMA_CROSS = 0.05
SAMPLES = 524288
LANES = 128
COARSE = 8
FOLDED = SAMPLES // COARSE
OUTER = FOLDED // LANES
REACH = HALO // LANES
FIELD_ROWS = 2 * 3 * 64
SMEM = pltpu.SMEM
VMEM = pltpu.VMEM


def split_np(matrix):
    upper = matrix.astype(ml_dtypes.bfloat16)
    lower = (matrix - upper.astype(np.float64)).astype(ml_dtypes.bfloat16)
    return np.stack([upper, lower])


def roots(numerators, period):
    angles = (numerators % period) * (2.0 * np.pi / period)
    return np.cos(angles), np.sin(angles)


@functools.cache
def inner_table():
    lane_ids = np.arange(LANES, dtype=np.int64)
    cosine, sine = roots(lane_ids[:, None] * lane_ids[None, :], LANES)
    forward = np.block([[cosine, -sine], [sine, cosine]])
    return np.stack([split_np(forward), split_np(forward.T)])


@functools.cache
def tables():
    outer_ids = np.arange(OUTER, dtype=np.int64)
    lane_ids = np.arange(LANES, dtype=np.int64)
    residues = np.arange(COARSE, dtype=np.int64)
    half = OUTER // 2
    half_ids = np.arange(half, dtype=np.int64)
    cosine, sine = roots(half_ids[:, None] * half_ids[None, :], half)
    outer = np.stack([split_np(cosine), split_np(sine)])
    middle = np.stack(roots(half_ids[:, None] + 0 * lane_ids[None, :], OUTER))
    order = np.concatenate([outer_ids[0::2], outer_ids[1::2]])
    turn = np.stack(roots(order[:, None] * lane_ids[None, :], FOLDED))
    around = np.concatenate([outer_ids, np.arange(-REACH, 0), OUTER + np.arange(REACH)])
    time_ids = LANES * around[:, None] + lane_ids[None, :]
    shift = np.stack(roots(residues[:, None, None] * time_ids[None], SAMPLES), axis=1)
    freq_ids = residues[:, None, None] + COARSE * (
        order[None, :, None] + OUTER * lane_ids[None, None, :]
    )
    signed_ids = np.where(freq_ids < SAMPLES // 2, freq_ids, freq_ids - SAMPLES)
    response = np.stack(roots(signed_ids * signed_ids, 4 * SAMPLES), axis=1) / SAMPLES
    response = np.pad(response, ((0, 0), (0, 0), (0, 2 * REACH), (0, 0)))
    by_residue = np.concatenate([shift, response], axis=1).astype(np.float32)
    return outer, middle.astype(np.float32), turn.astype(np.float32), by_residue


def radix_eight(parts, sign):
    half = np.float32(np.sqrt(0.5))

    def add(a, b):
        return a[0] + b[0], a[1] + b[1]

    def sub(a, b):
        return a[0] - b[0], a[1] - b[1]

    def quarter(a):
        return (-sign * a[1], sign * a[0])

    def eighth(a):
        return (half * (a[0] - sign * a[1]), half * (a[1] + sign * a[0]))

    def four(a, b, c, d):
        even_sum, even_diff = add(a, c), sub(a, c)
        odd_sum, odd_diff = add(b, d), quarter(sub(b, d))
        return (
            add(even_sum, odd_sum),
            add(even_diff, odd_diff),
            sub(even_sum, odd_sum),
            sub(even_diff, odd_diff),
        )

    even = four(*(add(parts[i], parts[i + 4]) for i in range(4)))
    diffs = [sub(parts[i], parts[i + 4]) for i in range(4)]
    odd = four(
        diffs[0], eighth(diffs[1]), quarter(diffs[2]), quarter(eighth(diffs[3]))
    )
    return [pair for both in zip(even, odd) for pair in both]


def head_kernel(in_ref, out_ref):
    for group in range(COARSE):
        for row in range(3):
            chan, pol = divmod(3 * group + row, 2)
            for part in range(2):
                out_ref[group, part, row] = in_ref[part, chan, pl.ds(pol, 64, stride=2), :]


def head(launched):
    vmem = pl.BlockSpec(memory_space=VMEM)
    return pl.pallas_call(
        head_kernel,
        in_specs=[vmem],
        out_specs=vmem,
        out_shape=jax.ShapeDtypeStruct((COARSE, 2, 3, 64, LANES), jnp.float32),
        name="head",
    )(interleaved(launched))


def interleaved(values):
    lead = values.shape[:-2]
    blocks = values.shape[-1] // LANES
    values = values.reshape(lead + (2, blocks, LANES))
    return jnp.swapaxes(values, -3, -2).reshape(lead + (2 * blocks, LANES))


def fold_kernel(in_ref, out_ref):
    rows = 8
    for row in range(in_ref.shape[2]):
        for step in range(in_ref.shape[3] // rows):
            at = slice(step * rows, step * rows + rows)
            parts = [(in_ref[i, 0, row, at, :], in_ref[i, 1, row, at, :]) for i in range(COARSE)]
            for i, pair in enumerate(radix_eight(parts, -1)):
                out_ref[i, 0, row, at, :] = pair[0]
                out_ref[i, 1, row, at, :] = pair[1]


def fold(values):
    spec = pl.BlockSpec((COARSE, 2, 3, 32, LANES), lambda k: (0, 0, 0, k, 0))
    return pl.pallas_call(
        fold_kernel,
        grid=(2,),
        in_specs=[spec],
        out_specs=spec,
        out_shape=jax.ShapeDtypeStruct(values.shape, jnp.float32),
        name="fold",
    )(values)


def halves(values):
    upper = values.astype(jnp.bfloat16)
    lower = (values - upper.astype(jnp.float32)).astype(jnp.bfloat16)
    return upper, lower


def dot(left, right):
    return jnp.dot(left, right, preferred_element_type=jnp.float32)


def triple(left, right):
    return dot(left[0], right[0]) + (dot(left[0], right[1]) + dot(left[1], right[0]))


def turned(real, imag, cosine, sine, sign):
    if sign > 0:
        return real * cosine - imag * sine, imag * cosine + real * sine
    return real * cosine + imag * sine, imag * cosine - real * sine


def packed(real, imag):
    return halves(jnp.concatenate([real, imag], axis=1))


def outer_dft(outer_ref, first, second, sign):
    values = halves(jnp.concatenate([*first, *second], axis=1))
    by_cos = triple((outer_ref[0, 0], outer_ref[0, 1]), values)
    by_sin = triple((outer_ref[1, 0], outer_ref[1, 1]), values)
    found = []
    for low in (0, 2 * LANES):
        cos_real, cos_imag = by_cos[:, low : low + LANES], by_cos[:, low + LANES : low + 2 * LANES]
        sin_real, sin_imag = by_sin[:, low : low + LANES], by_sin[:, low + LANES : low + 2 * LANES]
        if sign > 0:
            found.append((cos_real - sin_imag, cos_imag + sin_real))
        else:
            found.append((cos_real + sin_imag, cos_imag - sin_real))
    return found


def disperse_kernel(in_ref, outer_ref, inner_ref, middle_ref, turn_ref, own_ref, out_ref, work):
    half = OUTER // 2
    middle = (middle_ref[0], middle_ref[1])
    for row in range(in_ref.shape[2]):
        real = in_ref[:, 0, row].reshape(OUTER, LANES)
        imag = in_ref[:, 1, row].reshape(OUTER, LANES)
        real, imag = turned(real, imag, own_ref[0, :OUTER], own_ref[1, :OUTER], -1)
        even = (real[:half] + real[half:], imag[:half] + imag[half:])
        odd = turned(real[:half] - real[half:], imag[:half] - imag[half:], *middle, -1)
        even, odd = outer_dft(outer_ref, even, odd, -1)
        real, imag = (jnp.concatenate([even[k], odd[k]], axis=0) for k in range(2))
        values = packed(*turned(real, imag, turn_ref[0], turn_ref[1], -1))
        both = triple(values, (inner_ref[0, 0], inner_ref[0, 1]))
        real, imag = turned(
            both[:, :LANES], both[:, LANES:], own_ref[2, :OUTER], own_ref[3, :OUTER], 1
        )
        both = triple(packed(real, imag), (inner_ref[1, 0], inner_ref[1, 1]))
        real, imag = turned(both[:, :LANES], both[:, LANES:], turn_ref[0], turn_ref[1], 1)
        even, odd = outer_dft(
            outer_ref, (real[:half], imag[:half]), (real[half:], imag[half:]), 1
        )
        odd = turned(*odd, *middle, 1)
        for part in range(2):
            work[part, :half] = even[part] + odd[part]
            work[part, half:OUTER] = even[part] - odd[part]
            work[part, OUTER : OUTER + REACH] = work[part, OUTER - REACH : OUTER]
            work[part, OUTER + REACH :] = work[part, :REACH]
        work[0], work[1] = turned(work[0], work[1], own_ref[0], own_ref[1], 1)
        for group in range(8):
            low, high = 64 * group, 64 * group + 64
            before = low - REACH if group else OUTER
            after = high if group < 7 else OUTER + REACH
            for part in range(2):
                out_ref[group, part, row, :64] = work[part, low:high]
                out_ref[group, part, row, 64 : 64 + REACH] = work[part, before : before + REACH]
                out_ref[group, part, row, 64 + REACH :] = work[part, after : after + REACH]


def disperse(values, own):
    outer, middle, turn, _ = tables()
    vmem = pl.BlockSpec(memory_space=VMEM)
    shape = values.shape[:3] + (64 + 2 * REACH, LANES)
    return pl.pallas_call(
        disperse_kernel,
        in_specs=[vmem] * 6,
        out_specs=vmem,
        out_shape=jax.ShapeDtypeStruct(shape, jnp.float32),
        scratch_shapes=[VMEM((2, OUTER + 2 * REACH, LANES), jnp.float32)],
        compiler_params=pltpu.CompilerParams(vmem_limit_bytes=32 * 1024 * 1024),
        name="disperse",
    )(values, outer, inner_table(), middle, turn, own)


def field_rows(part, row):
    low = (3 * part + row) * 64
    return slice(low, low + 64)


def unfold_kernel(place_ref, in_ref, out_ref):
    rows = 8
    even = place_ref[0] % 2 == 0
    for step in range(in_ref.shape[3] // rows):
        at = slice(step * rows, step * rows + rows)
        squares = []
        for row in range(3):
            parts = [(in_ref[i, 0, row, at, :], in_ref[i, 1, row, at, :]) for i in range(COARSE)]
            results = radix_eight(parts, 1)
            if step < 8:
                for i, pair in enumerate(results):
                    for part in range(2):
                        low = field_rows(part, row).start + step * rows
                        out_ref[i, low : low + rows, :] = pair[part]
            else:
                squares.append([real * real + imag * imag for real, imag in results])
        if step == 8:
            for i in range(COARSE):
                middle = squares[1][i]
                nothing = jnp.zeros_like(middle)
                first = squares[0][i] + jnp.where(even, middle, nothing)
                second = squares[2][i] + jnp.where(even, nothing, middle)
                out_ref[i, FIELD_ROWS : FIELD_ROWS + rows, :] = first
                out_ref[i, FIELD_ROWS + rows :, :] = second


def unfold(values, place):
    vmem = pl.BlockSpec(memory_space=VMEM)
    shape = (COARSE, FIELD_ROWS + 16, LANES)
    return pl.pallas_call(
        unfold_kernel,
        in_specs=[pl.BlockSpec(memory_space=SMEM), vmem],
        out_specs=vmem,
        out_shape=jax.ShapeDtypeStruct(shape, jnp.float32),
        compiler_params=pltpu.CompilerParams(vmem_limit_bytes=24 * 1024 * 1024),
        name="unfold",
    )(place, values)


def fields_of(held, chan):
    found = []
    for pol in range(2):
        group, row = divmod(2 * chan + pol, 3)
        found.append((held[group, field_rows(0, row), :], held[group, field_rows(1, row), :]))
    return found


def slide_kernel(held, table_ref, out_ref, extended):
    groups, local_chan, taken, _ = out_ref.shape
    table = table_ref[...]
    span = 64 + 2 * REACH
    for chan in range(local_chan):
        powers = sum(real * real + imag * imag for real, imag in fields_of(held, chan))
        extended[chan, REACH : REACH + 64, :] = powers
        pair, place = divmod(chan, 3)
        low = FIELD_ROWS + (place + 1) // 2 * 8
        around = held[2 * pair + place // 2, low : low + 8, :]
        if place == 1:
            around = around + held[2 * pair + 1, FIELD_ROWS : FIELD_ROWS + 8, :]
        extended[chan, :REACH, :] = around[:REACH]
        extended[chan, 64 + REACH : span, :] = around[REACH:]
        extended[chan, span:, :] = jnp.zeros_like(around)
        both = jnp.concatenate(
            [extended[chan, :span, :], extended[chan, 1 : span + 1, :]], axis=1
        )
        upper, lower = halves(both)
        sliding = dot(upper, table) + dot(lower, table)
        for group in range(groups):
            out_ref[group, chan] = sliding[8 * group : 8 * group + taken]


def slide(fields, groups, local_chan):
    rows_idx = np.arange(2 * LANES)[:, None]
    cols_idx = np.arange(LANES)[None, :]
    table = ((rows_idx >= cols_idx) & (rows_idx < cols_idx + LANES)).astype(ml_dtypes.bfloat16)
    vmem = pl.BlockSpec(memory_space=VMEM)
    return pl.pallas_call(
        slide_kernel,
        in_specs=[vmem, vmem],
        out_specs=vmem,
        out_shape=jax.ShapeDtypeStruct((groups, local_chan, 16, LANES), jnp.float32),
        scratch_shapes=[VMEM((local_chan, 64 + 2 * REACH + 8, LANES), jnp.float32)],
        compiler_params=pltpu.CompilerParams(vmem_limit_bytes=24 * 1024 * 1024),
        name="slide",
    )(fields, table)


def cross_kernel(starts_ref, lengths_ref, in_ref, out_ref, gathered, weights, uppers, lowers):
    channels = starts_ref.shape[0]
    shifts = weights.shape[2] // LANES
    own = out_ref.shape[1]
    taken = in_ref.shape[0] // channels
    starts, lengths = starts_ref[...], lengths_ref[...]
    inverse = 1.0 / lengths.astype(jnp.float32)
    others = lax.broadcasted_iota(jnp.int32, starts.shape, 0) != lax.broadcasted_iota(
        jnp.int32, starts.shape, 1
    )
    nothing = jnp.zeros_like(inverse)
    weights[...] = jnp.zeros_like(weights)
    for shift in range(shifts):
        offset = LANES * shift - HALO
        inside = (starts <= offset) & (offset + LANES <= starts + lengths)
        values = halves(jnp.where(inside & others, inverse, nothing))
        for k in range(2):
            weights[k, :, shift * LANES : shift * LANES + channels] = values[k]
    gathered[...] = jnp.zeros_like(gathered)
    for step in range(taken - 1):
        gathered[:channels, :] = in_ref[pl.ds(step, channels, stride=taken), :]
        at = slice(step * LANES, (step + 1) * LANES)
        uppers[at, :], lowers[at, :] = halves(gathered[...])
    pair_weights = (weights[0], weights[1])
    for step in range(0, own, 2):

        def pair(ref):
            low, depth = step * LANES, shifts * LANES
            return jnp.concatenate(
                [ref[low : low + depth, :], ref[low + LANES : low + LANES + depth, :]], axis=1
            )

        both = triple(pair_weights, (pair(uppers), pair(lowers)))
        out_ref[:, step, :] = both[:, :LANES]
        out_ref[:, step + 1, :] = both[:, LANES:]


def cross(starts, lengths, blocks, own):
    channels = starts.shape[0]
    shifts = 2 * HALO // LANES
    taken = blocks.shape[2]
    vmem = pl.BlockSpec(memory_space=VMEM)
    return pl.pallas_call(
        cross_kernel,
        in_specs=[vmem] * 3,
        out_specs=vmem,
        out_shape=jax.ShapeDtypeStruct((channels, own, LANES), jnp.float32),
        scratch_shapes=[
            VMEM((LANES, LANES), jnp.float32),
            VMEM((2, channels, shifts * LANES), jnp.bfloat16),
            VMEM(((taken - 1) * LANES, LANES), jnp.bfloat16),
            VMEM(((taken - 1) * LANES, LANES), jnp.bfloat16),
        ],
        name="cross",
    )(starts, lengths, blocks.reshape(-1, LANES))


def cosine_and_sine(angles):
    turns = jnp.floor(angles * np.float32(2.0 / np.pi) + 0.5)
    rest = ((angles - turns * 1.5703125) - turns * 4.837512969970703125e-4) - turns * np.float32(
        7.54978995489188216e-8
    )
    square = rest * rest
    sine = rest + rest * square * (
        -1.6666654611e-1 + square * (8.3321608736e-3 + square * -1.9515295891e-4)
    )
    cosine = (1.0 - 0.5 * square) + square * square * (
        4.166664568298827e-2 + square * (-1.388731625493765e-3 + square * 2.443315711809948e-5)
    )
    quadrant = turns.astype(jnp.int32) & 3
    swap = (quadrant & 1) == 1
    near, far = jnp.where(swap, sine, cosine), jnp.where(swap, cosine, sine)
    turned = (quadrant == 1) | (quadrant == 2)
    return jnp.where(turned, -near, near), jnp.where(quadrant >= 2, -far, far)


def tail_kernel(held, cross_ref, noise_ref, out_ref):
    for chan in range(out_ref.shape[1]):
        fields = fields_of(held, chan)
        others = cross_ref[:, chan].reshape(64, LANES)
        powers = sum(real * real + imag * imag for real, imag in fields)
        cosine, sine = cosine_and_sine(GAMMA_SELF * powers + GAMMA_CROSS * others)
        for pol, (real, imag) in enumerate(fields):
            at = pl.ds(pol, 64, stride=2)
            out_ref[0, chan, at, :] = cosine * real - sine * imag
            out_ref[1, chan, at, :] = cosine * imag + sine * real
        for part in range(2):
            out_ref[part, chan] = out_ref[part, chan] + noise_ref[part, chan].astype(jnp.float32)


def tail(fields, cross_sum, amp_noise):
    local_chan = cross_sum.shape[1]
    vmem = pl.BlockSpec(memory_space=VMEM)
    received = pl.pallas_call(
        tail_kernel,
        in_specs=[vmem] * 3,
        out_specs=vmem,
        out_shape=jax.ShapeDtypeStruct((2, local_chan, 128, LANES), jnp.float32),
        compiler_params=pltpu.CompilerParams(vmem_limit_bytes=24 * 1024 * 1024),
        name="tail",
    )(fields, cross_sum, interleaved(amp_noise))
    received = received.reshape(2, local_chan, 64, 2, LANES)
    return jnp.swapaxes(received, 2, 3).reshape(amp_noise.shape)


def exchange(values, axis):
    return lax.all_to_all(values, axis, 0, 0, tiled=True)


def per_device(launched, amp_noise, window_start, window_length):
    local_chan = launched.shape[1]
    groups = lax.axis_size("chan")
    place = lax.axis_index("j").astype(jnp.int32).reshape(1)
    own_tables = lax.dynamic_index_in_dim(
        jnp.asarray(tables()[3]), lax.axis_index("i"), 0, keepdims=False
    )
    values = exchange(head(launched), "j")
    values = exchange(fold(values), "i")
    values = exchange(disperse(values, own_tables), "i")
    fields = exchange(unfold(values, place), "j")
    blocks = exchange(slide(fields, groups, local_chan), "chan")
    cross_sum = cross(window_start, window_length, blocks, 64 // groups)
    cross_sum = exchange(cross_sum.reshape(groups, local_chan, -1, LANES), "chan")
    return tail(fields, cross_sum, amp_noise)


def solution(mesh):
    split = Mesh(mesh.devices.reshape(mesh.shape["chan"], COARSE, -1), ("chan", "j", "i"))
    fields = P(None, "chan", None, ("j", "i"))
    return jax.shard_map(
        per_device,
        mesh=split,
        in_specs=(fields, fields, P(), P()),
        out_specs=fields,
        check_vma=False,
    )
```

```python
import functools

import jax
import jax.numpy as jnp
import ml_dtypes
import numpy as np
from jax import lax
from jax.experimental import pallas as pl
from jax.experimental.pallas import tpu as pltpu
from jax.sharding import Mesh
from jax.sharding import PartitionSpec as P

HALO = 512
GAMMA_SELF = 0.1
GAMMA_CROSS = 0.05
SAMPLES = 524288
LANES = 128
COARSE = 8
FOLDED = SAMPLES // COARSE
OUTER = FOLDED // LANES
REACH = HALO // LANES
WHOLE = 8
FIELD_ROWS = 2 * 3 * 64
SMEM = pltpu.SMEM
VMEM = pltpu.VMEM


def split_np(matrix):
    upper = matrix.astype(ml_dtypes.bfloat16)
    lower = (matrix - upper.astype(np.float64)).astype(ml_dtypes.bfloat16)
    return np.stack([upper, lower])


def roots(numerators, period):
    angles = (numerators % period) * (2.0 * np.pi / period)
    return np.cos(angles), np.sin(angles)


@functools.cache
def inner_table():
    lane_ids = np.arange(LANES, dtype=np.int64)
    cosine, sine = roots(lane_ids[:, None] * lane_ids[None, :], LANES)
    forward = np.block([[cosine, -sine], [sine, cosine]])
    return np.stack([split_np(forward), split_np(forward.T)])


@functools.cache
def tables():
    outer_ids = np.arange(OUTER, dtype=np.int64)
    lane_ids = np.arange(LANES, dtype=np.int64)
    residues = np.arange(COARSE, dtype=np.int64)
    half = OUTER // 2
    half_ids = np.arange(half, dtype=np.int64)
    cosine, sine = roots(half_ids[:, None] * half_ids[None, :], half)
    outer = np.stack([split_np(cosine), split_np(sine)])
    middle = np.stack(roots(half_ids[:, None] + 0 * lane_ids[None, :], OUTER))
    order = np.concatenate([outer_ids[0::2], outer_ids[1::2]])
    turn = np.stack(roots(order[:, None] * lane_ids[None, :], FOLDED))
    around = np.concatenate([outer_ids, np.arange(-REACH, 0), OUTER + np.arange(REACH)])
    time_ids = LANES * around[:, None] + lane_ids[None, :]
    shift = np.stack(roots(residues[:, None, None] * time_ids[None], SAMPLES), axis=1)
    freq_ids = residues[:, None, None] + COARSE * (
        order[None, :, None] + OUTER * lane_ids[None, None, :]
    )
    signed_ids = np.where(freq_ids < SAMPLES // 2, freq_ids, freq_ids - SAMPLES)
    response = np.stack(roots(signed_ids * signed_ids, 4 * SAMPLES), axis=1) / SAMPLES
    response = np.pad(response, ((0, 0), (0, 0), (0, 2 * REACH), (0, 0)))
    by_residue = np.concatenate([shift, response], axis=1).astype(np.float32)
    return outer, middle.astype(np.float32), turn.astype(np.float32), by_residue


def radix_eight(parts, sign):
    half = np.float32(np.sqrt(0.5))

    def add(a, b):
        return a[0] + b[0], a[1] + b[1]

    def sub(a, b):
        return a[0] - b[0], a[1] - b[1]

    def quarter(a):
        return (-sign * a[1], sign * a[0])

    def eighth(a):
        return (half * (a[0] - sign * a[1]), half * (a[1] + sign * a[0]))

    def four(a, b, c, d):
        even_sum, even_diff = add(a, c), sub(a, c)
        odd_sum, odd_diff = add(b, d), quarter(sub(b, d))
        return (
            add(even_sum, odd_sum),
            add(even_diff, odd_diff),
            sub(even_sum, odd_sum),
            sub(even_diff, odd_diff),
        )

    even = four(*(add(parts[i], parts[i + 4]) for i in range(4)))
    diffs = [sub(parts[i], parts[i + 4]) for i in range(4)]
    odd = four(
        diffs[0], eighth(diffs[1]), quarter(diffs[2]), quarter(eighth(diffs[3]))
    )
    return [pair for both in zip(even, odd) for pair in both]


def rows_of(group):
    return ((group, 0), (group, 1), (WHOLE + group // 2, group % 2))


def head_kernel(in_ref, out_ref):
    for group in range(COARSE):
        for row, (chan, pol) in enumerate(rows_of(group)):
            for part in range(2):
                out_ref[group, part, row] = in_ref[part, chan, pl.ds(pol, 64, stride=2), :]


def head(launched):
    vmem = pl.BlockSpec(memory_space=VMEM)
    return pl.pallas_call(
        head_kernel,
        in_specs=[vmem],
        out_specs=vmem,
        out_shape=jax.ShapeDtypeStruct((COARSE, 2, 3, 64, LANES), jnp.float32),
        name="head",
    )(interleaved(launched))


def interleaved(values):
    lead = values.shape[:-2]
    blocks = values.shape[-1] // LANES
    values = values.reshape(lead + (2, blocks, LANES))
    return jnp.swapaxes(values, -3, -2).reshape(lead + (2 * blocks, LANES))


def fold_kernel(in_ref, out_ref):
    rows = 8
    for row in range(in_ref.shape[2]):
        for step in range(in_ref.shape[3] // rows):
            at = slice(step * rows, step * rows + rows)
            parts = [(in_ref[i, 0, row, at, :], in_ref[i, 1, row, at, :]) for i in range(COARSE)]
            for i, pair in enumerate(radix_eight(parts, -1)):
                out_ref[i, 0, row, at, :] = pair[0]
                out_ref[i, 1, row, at, :] = pair[1]


def fold(values):
    spec = pl.BlockSpec((COARSE, 2, 3, 32, LANES), lambda k: (0, 0, 0, k, 0))
    return pl.pallas_call(
        fold_kernel,
        grid=(2,),
        in_specs=[spec],
        out_specs=spec,
        out_shape=jax.ShapeDtypeStruct(values.shape, jnp.float32),
        name="fold",
    )(values)


def halves(values):
    upper = values.astype(jnp.bfloat16)
    lower = (values - upper.astype(jnp.float32)).astype(jnp.bfloat16)
    return upper, lower


def dot(left, right):
    return jnp.dot(left, right, preferred_element_type=jnp.float32)


def triple(left, right):
    return dot(left[0], right[0]) + (dot(left[0], right[1]) + dot(left[1], right[0]))


def turned(real, imag, cosine, sine, sign):
    if sign > 0:
        return real * cosine - imag * sine, imag * cosine + real * sine
    return real * cosine + imag * sine, imag * cosine - real * sine


def packed(real, imag):
    return halves(jnp.concatenate([real, imag], axis=1))


def outer_dft(dft_ref, first, second, sign):
    values = halves(jnp.concatenate([*first, *second], axis=1))
    by_cos = triple((dft_ref[0, 0], dft_ref[0, 1]), values)
    by_sin = triple((dft_ref[1, 0], dft_ref[1, 1]), values)
    found = []
    for low in (0, 2 * LANES):
        cos_real, cos_imag = by_cos[:, low : low + LANES], by_cos[:, low + LANES : low + 2 * LANES]
        sin_real, sin_imag = by_sin[:, low : low + LANES], by_sin[:, low + LANES : low + 2 * LANES]
        if sign > 0:
            found.append((cos_real - sin_imag, cos_imag + sin_real))
        else:
            found.append((cos_real + sin_imag, cos_imag - sin_real))
    return found


def disperse_kernel(in_ref, dft_ref, middle_ref, turn_ref, own_ref, out_ref, work):
    half = OUTER // 2
    middle = (middle_ref[0], middle_ref[1])
    for row in range(in_ref.shape[2]):
        real = in_ref[:, 0, row].reshape(OUTER, LANES)
        imag = in_ref[:, 1, row].reshape(OUTER, LANES)
        real, imag = turned(real, imag, own_ref[0, :OUTER], own_ref[1, :OUTER], -1)
        even = (real[:half] + real[half:], imag[:half] + imag[half:])
        odd = turned(real[:half] - real[half:], imag[:half] - imag[half:], *middle, -1)
        even, odd = outer_dft(dft_ref, even, odd, -1)
        real, imag = (jnp.concatenate([even[k], odd[k]], axis=0) for k in range(2))
        values = packed(*turned(real, imag, turn_ref[0], turn_ref[1], -1))
        both = triple(values, (dft_ref[2, 0], dft_ref[2, 1]))
        real, imag = turned(
            both[:, :LANES], both[:, LANES:], own_ref[2, :OUTER], own_ref[3, :OUTER], 1
        )
        both = triple(packed(real, imag), (dft_ref[3, 0], dft_ref[3, 1]))
        real, imag = turned(both[:, :LANES], both[:, LANES:], turn_ref[0], turn_ref[1], 1)
        even, odd = outer_dft(
            dft_ref, (real[:half], imag[:half]), (real[half:], imag[half:]), 1
        )
        odd = turned(*odd, *middle, 1)
        for part in range(2):
            work[part, :half] = even[part] + odd[part]
            work[part, half:OUTER] = even[part] - odd[part]
            work[part, OUTER : OUTER + REACH] = work[part, OUTER - REACH : OUTER]
            work[part, OUTER + REACH :] = work[part, :REACH]
        work[0], work[1] = turned(work[0], work[1], own_ref[0], own_ref[1], 1)
        for group in range(8):
            low, high = 64 * group, 64 * group + 64
            before = low - REACH if group else OUTER
            after = high if group < 7 else OUTER + REACH
            for part in range(2):
                out_ref[group, part, row, :64] = work[part, low:high]
                out_ref[group, part, row, 64 : 64 + REACH] = work[part, before : before + REACH]
                out_ref[group, part, row, 64 + REACH :] = work[part, after : after + REACH]


def disperse(values, own):
    outer, middle, turn, _ = tables()
    vmem = pl.BlockSpec(memory_space=VMEM)
    shape = values.shape[:3] + (64 + 2 * REACH, LANES)
    return pl.pallas_call(
        disperse_kernel,
        in_specs=[vmem] * 5,
        out_specs=vmem,
        out_shape=jax.ShapeDtypeStruct(shape, jnp.float32),
        scratch_shapes=[VMEM((2, OUTER + 2 * REACH, LANES), jnp.float32)],
        compiler_params=pltpu.CompilerParams(vmem_limit_bytes=32 * 1024 * 1024),
        name="disperse",
    )(values, np.concatenate([outer, inner_table()]), middle, turn, own)


def field_rows(part, row):
    low = (3 * part + row) * 64
    return slice(low, low + 64)


def unfold_kernel(in_ref, out_ref):
    rows = 8
    for step in range(in_ref.shape[3] // rows):
        at = slice(step * rows, step * rows + rows)
        squares = []
        for row in range(3):
            parts = [(in_ref[i, 0, row, at, :], in_ref[i, 1, row, at, :]) for i in range(COARSE)]
            results = radix_eight(parts, 1)
            if step < 8:
                for i, pair in enumerate(results):
                    for part in range(2):
                        low = field_rows(part, row).start + step * rows
                        out_ref[i, low : low + rows, :] = pair[part]
            else:
                squares.append([real * real + imag * imag for real, imag in results])
        if step == 8:
            for i in range(COARSE):
                out_ref[i, FIELD_ROWS : FIELD_ROWS + rows, :] = squares[0][i] + squares[1][i]
                out_ref[i, FIELD_ROWS + rows :, :] = squares[2][i]


def unfold(values):
    vmem = pl.BlockSpec(memory_space=VMEM)
    return pl.pallas_call(
        unfold_kernel,
        in_specs=[vmem],
        out_specs=vmem,
        out_shape=jax.ShapeDtypeStruct((COARSE, FIELD_ROWS + 4 * REACH, LANES), jnp.float32),
        compiler_params=pltpu.CompilerParams(vmem_limit_bytes=24 * 1024 * 1024),
        name="unfold",
    )(values)


def fields_of(held, chan):
    found = []
    for pol in range(2):
        group, row = (chan, pol) if chan < WHOLE else (2 * (chan - WHOLE) + pol, 2)
        found.append((held[group, field_rows(0, row), :], held[group, field_rows(1, row), :]))
    return found


def powers_around(held, chan):
    if chan < WHOLE:
        return held[chan, FIELD_ROWS : FIELD_ROWS + 2 * REACH, :]
    group = 2 * (chan - WHOLE)
    return held[group, FIELD_ROWS + 2 * REACH :, :] + held[group + 1, FIELD_ROWS + 2 * REACH :, :]


def sliding_sums(powers, around, table, extended):
    span = 64 + 2 * REACH
    extended[REACH : REACH + 64, :] = powers
    extended[:REACH, :] = around[:REACH]
    extended[64 + REACH : span, :] = around[REACH:]
    extended[span:, :] = jnp.zeros_like(around)
    both = jnp.concatenate([extended[:span, :], extended[1 : span + 1, :]], axis=1)
    upper, lower = halves(both)
    return dot(upper, table) + dot(lower, table)


def total(fields):
    return sum(real * real + imag * imag for real, imag in fields)


def slide_kernel(held, table_ref, out_ref, extended):
    groups, local_chan, taken, _ = out_ref.shape
    table = table_ref[...]
    for chan in range(local_chan):
        powers = total(fields_of(held, chan))
        around = powers_around(held, chan)
        sliding = sliding_sums(powers, around, table, extended.at[chan])
        for group in range(groups):
            out_ref[group, chan] = sliding[8 * group : 8 * group + taken]


def slide_table():
    rows_idx = np.arange(2 * LANES)[:, None]
    cols_idx = np.arange(LANES)[None, :]
    return ((rows_idx >= cols_idx) & (rows_idx < cols_idx + LANES)).astype(ml_dtypes.bfloat16)


def slide(fields, groups, local_chan):
    vmem = pl.BlockSpec(memory_space=VMEM)
    return pl.pallas_call(
        slide_kernel,
        in_specs=[vmem, vmem],
        out_specs=vmem,
        out_shape=jax.ShapeDtypeStruct((groups, local_chan, 16, LANES), jnp.float32),
        scratch_shapes=[VMEM((local_chan, 64 + 2 * REACH + 8, LANES), jnp.float32)],
        compiler_params=pltpu.CompilerParams(vmem_limit_bytes=24 * 1024 * 1024),
        name="slide",
    )(fields, slide_table())


def cross_kernel(starts_ref, lengths_ref, in_ref, out_ref, weights, uppers, lowers):
    channels = starts_ref.shape[0]
    shifts = 2 * HALO // LANES
    own = out_ref.shape[1]
    taken = in_ref.shape[0] // channels
    starts, lengths = starts_ref[...], lengths_ref[...]
    inverse = 1.0 / lengths.astype(jnp.float32)
    others = lax.broadcasted_iota(jnp.int32, starts.shape, 0) != lax.broadcasted_iota(
        jnp.int32, starts.shape, 1
    )
    nothing = jnp.zeros_like(inverse)
    for shift in range(shifts):
        offset = LANES * shift - HALO
        inside = (starts <= offset) & (offset + LANES <= starts + lengths)
        weights[:, shift * channels : (shift + 1) * channels] = jnp.where(
            inside & others, inverse, nothing
        )
    for step in range(taken - 1):
        at = slice(step * channels, (step + 1) * channels)
        uppers[at, :], lowers[at, :] = halves(in_ref[pl.ds(step, channels, stride=taken), :])
    pair_weights = halves(weights[...])
    for step in range(0, own, 2):

        def pair(ref):
            low, depth = step * channels, shifts * channels
            return jnp.concatenate(
                [ref[low : low + depth, :], ref[low + channels : low + channels + depth, :]],
                axis=1,
            )

        both = triple(pair_weights, (pair(uppers), pair(lowers)))
        out_ref[:, step, :] = both[:, :LANES]
        out_ref[:, step + 1, :] = both[:, LANES:]


def cross(starts, lengths, blocks, own):
    channels = starts.shape[0]
    shifts = 2 * HALO // LANES
    rows = (blocks.shape[2] - 1) * channels
    vmem = pl.BlockSpec(memory_space=VMEM)
    return pl.pallas_call(
        cross_kernel,
        in_specs=[vmem] * 3,
        out_specs=vmem,
        out_shape=jax.ShapeDtypeStruct((channels, own, LANES), jnp.float32),
        scratch_shapes=[
            VMEM((channels, shifts * channels), jnp.float32),
            VMEM((rows, LANES), jnp.bfloat16),
            VMEM((rows, LANES), jnp.bfloat16),
        ],
        name="cross",
    )(starts, lengths, blocks.reshape(-1, LANES))


def cosine_and_sine(angles):
    turns = jnp.floor(angles * np.float32(2.0 / np.pi) + 0.5)
    rest = ((angles - turns * 1.5703125) - turns * 4.837512969970703125e-4) - turns * np.float32(
        7.54978995489188216e-8
    )
    square = rest * rest
    sine = rest + rest * square * (
        -1.6666654611e-1 + square * (8.3321608736e-3 + square * -1.9515295891e-4)
    )
    cosine = (1.0 - 0.5 * square) + square * square * (
        4.166664568298827e-2 + square * (-1.388731625493765e-3 + square * 2.443315711809948e-5)
    )
    quadrant = turns.astype(jnp.int32) & 3
    swap = (quadrant & 1) == 1
    near, far = jnp.where(swap, sine, cosine), jnp.where(swap, cosine, sine)
    turned = (quadrant == 1) | (quadrant == 2)
    return jnp.where(turned, -near, near), jnp.where(quadrant >= 2, -far, far)


def tail_kernel(held, cross_ref, noise_ref, out_ref):
    for chan in range(out_ref.shape[1]):
        fields = fields_of(held, chan)
        others = cross_ref[:, chan].reshape(64, LANES)
        cosine, sine = cosine_and_sine(GAMMA_SELF * total(fields) + GAMMA_CROSS * others)
        for pol, (real, imag) in enumerate(fields):
            at = pl.ds(pol, 64, stride=2)
            out_ref[0, chan, at, :] = cosine * real - sine * imag
            out_ref[1, chan, at, :] = cosine * imag + sine * real
        for part in range(2):
            out_ref[part, chan] = out_ref[part, chan] + noise_ref[part, chan].astype(jnp.float32)


def tail(fields, cross_sum, amp_noise):
    local_chan = cross_sum.shape[1]
    vmem = pl.BlockSpec(memory_space=VMEM)
    received = pl.pallas_call(
        tail_kernel,
        in_specs=[vmem] * 3,
        out_specs=vmem,
        out_shape=jax.ShapeDtypeStruct((2, local_chan, 128, LANES), jnp.float32),
        compiler_params=pltpu.CompilerParams(vmem_limit_bytes=24 * 1024 * 1024),
        name="tail",
    )(fields, cross_sum, interleaved(amp_noise))
    received = received.reshape(2, local_chan, 64, 2, LANES)
    return jnp.swapaxes(received, 2, 3).reshape(amp_noise.shape)


def exchange(values, axis):
    return lax.all_to_all(values, axis, 0, 0, tiled=True)


def per_device(launched, amp_noise, window_start, window_length):
    local_chan = launched.shape[1]
    groups = lax.axis_size("chan")
    own_tables = lax.dynamic_index_in_dim(
        jnp.asarray(tables()[3]), lax.axis_index("i"), 0, keepdims=False
    )
    values = exchange(head(launched), "j")
    values = exchange(fold(values), "i")
    values = exchange(disperse(values, own_tables), "i")
    fields = exchange(unfold(values), "j")
    blocks = exchange(slide(fields, groups, local_chan), "chan")
    cross_sum = cross(window_start, window_length, blocks, 64 // groups)
    cross_sum = exchange(cross_sum.reshape(groups, local_chan, -1, LANES), "chan")
    return tail(fields, cross_sum, amp_noise)


def solution(mesh):
    split = Mesh(mesh.devices.reshape(mesh.shape["chan"], COARSE, -1), ("chan", "j", "i"))
    fields = P(None, "chan", None, ("j", "i"))
    return jax.shard_map(
        per_device,
        mesh=split,
        in_specs=(fields, fields, P(), P()),
        out_specs=fields,
        check_vma=False,
    )
```

```python
import functools

import jax
import jax.numpy as jnp
import ml_dtypes
import numpy as np
from jax import lax
from jax.experimental import pallas as pl
from jax.experimental.pallas import tpu as pltpu
from jax.sharding import Mesh
from jax.sharding import PartitionSpec as P

HALO = 512
GAMMA_SELF = 0.1
GAMMA_CROSS = 0.05
SAMPLES = 524288
LANES = 128
COARSE = 8
FOLDED = SAMPLES // COARSE
OUTER = FOLDED // LANES
REACH = HALO // LANES
WHOLE = 8
GROUP = 8
TAKEN = 64 // GROUP + 1
FIELD_ROWS = 2 * 3 * 64
SMEM = pltpu.SMEM
VMEM = pltpu.VMEM


def split_np(matrix):
    upper = matrix.astype(ml_dtypes.bfloat16)
    lower = (matrix - upper.astype(np.float64)).astype(ml_dtypes.bfloat16)
    return np.stack([upper, lower])


def roots(numerators, period):
    angles = (numerators % period) * (2.0 * np.pi / period)
    return np.cos(angles), np.sin(angles)


@functools.cache
def inner_table():
    lane_ids = np.arange(LANES, dtype=np.int64)
    cosine, sine = roots(lane_ids[:, None] * lane_ids[None, :], LANES)
    forward = np.block([[cosine, -sine], [sine, cosine]])
    return np.stack([split_np(forward), split_np(forward.T)])


@functools.cache
def tables():
    outer_ids = np.arange(OUTER, dtype=np.int64)
    lane_ids = np.arange(LANES, dtype=np.int64)
    residues = np.arange(COARSE, dtype=np.int64)
    half = OUTER // 2
    half_ids = np.arange(half, dtype=np.int64)
    cosine, sine = roots(half_ids[:, None] * half_ids[None, :], half)
    outer = np.stack([split_np(cosine), split_np(sine)])
    middle = np.stack(roots(half_ids[:, None] + 0 * lane_ids[None, :], OUTER))
    order = np.concatenate([outer_ids[0::2], outer_ids[1::2]])
    turn = np.stack(roots(order[:, None] * lane_ids[None, :], FOLDED))
    around = np.concatenate([outer_ids, np.arange(-REACH, 0), OUTER + np.arange(REACH)])
    time_ids = LANES * around[:, None] + lane_ids[None, :]
    shift = np.stack(roots(residues[:, None, None] * time_ids[None], SAMPLES), axis=1)
    freq_ids = residues[:, None, None] + COARSE * (
        order[None, :, None] + OUTER * lane_ids[None, None, :]
    )
    signed_ids = np.where(freq_ids < SAMPLES // 2, freq_ids, freq_ids - SAMPLES)
    response = np.stack(roots(signed_ids * signed_ids, 4 * SAMPLES), axis=1) / SAMPLES
    response = np.pad(response, ((0, 0), (0, 0), (0, 2 * REACH), (0, 0)))
    by_residue = np.concatenate([shift, response], axis=1).astype(np.float32)
    return outer, middle.astype(np.float32), turn.astype(np.float32), by_residue


def radix_eight(parts, sign):
    half = np.float32(np.sqrt(0.5))

    def add(a, b):
        return a[0] + b[0], a[1] + b[1]

    def sub(a, b):
        return a[0] - b[0], a[1] - b[1]

    def quarter(a):
        return (-sign * a[1], sign * a[0])

    def eighth(a):
        return (half * (a[0] - sign * a[1]), half * (a[1] + sign * a[0]))

    def four(a, b, c, d):
        even_sum, even_diff = add(a, c), sub(a, c)
        odd_sum, odd_diff = add(b, d), quarter(sub(b, d))
        return (
            add(even_sum, odd_sum),
            add(even_diff, odd_diff),
            sub(even_sum, odd_sum),
            sub(even_diff, odd_diff),
        )

    even = four(*(add(parts[i], parts[i + 4]) for i in range(4)))
    diffs = [sub(parts[i], parts[i + 4]) for i in range(4)]
    odd = four(
        diffs[0], eighth(diffs[1]), quarter(diffs[2]), quarter(eighth(diffs[3]))
    )
    return [pair for both in zip(even, odd) for pair in both]


def rows_of(group):
    return ((group, 0), (group, 1), (WHOLE + group // 2, group % 2))


def head_kernel(in_ref, out_ref):
    for group in range(COARSE):
        for row, (chan, pol) in enumerate(rows_of(group)):
            for part in range(2):
                out_ref[group, part, row] = in_ref[part, chan, pl.ds(pol, 64, stride=2), :]


def head(launched):
    vmem = pl.BlockSpec(memory_space=VMEM)
    return pl.pallas_call(
        head_kernel,
        in_specs=[vmem],
        out_specs=vmem,
        out_shape=jax.ShapeDtypeStruct((COARSE, 2, 3, 64, LANES), jnp.float32),
        name="head",
    )(interleaved(launched))


def interleaved(values):
    lead = values.shape[:-2]
    blocks = values.shape[-1] // LANES
    values = values.reshape(lead + (2, blocks, LANES))
    return jnp.swapaxes(values, -3, -2).reshape(lead + (2 * blocks, LANES))


def fold_kernel(in_ref, out_ref):
    rows = 8
    for row in range(in_ref.shape[2]):
        for step in range(in_ref.shape[3] // rows):
            at = slice(step * rows, step * rows + rows)
            parts = [(in_ref[i, 0, row, at, :], in_ref[i, 1, row, at, :]) for i in range(COARSE)]
            for i, pair in enumerate(radix_eight(parts, -1)):
                out_ref[i, 0, row, at, :] = pair[0]
                out_ref[i, 1, row, at, :] = pair[1]


def fold(values):
    spec = pl.BlockSpec((COARSE, 2, 3, 32, LANES), lambda k: (0, 0, 0, k, 0))
    return pl.pallas_call(
        fold_kernel,
        grid=(2,),
        in_specs=[spec],
        out_specs=spec,
        out_shape=jax.ShapeDtypeStruct(values.shape, jnp.float32),
        name="fold",
    )(values)


def halves(values):
    upper = values.astype(jnp.bfloat16)
    lower = (values - upper.astype(jnp.float32)).astype(jnp.bfloat16)
    return upper, lower


def dot(left, right):
    return jnp.dot(left, right, preferred_element_type=jnp.float32)


def triple(left, right):
    return dot(left[0], right[0]) + (dot(left[0], right[1]) + dot(left[1], right[0]))


def turned(real, imag, cosine, sine, sign):
    if sign > 0:
        return real * cosine - imag * sine, imag * cosine + real * sine
    return real * cosine + imag * sine, imag * cosine - real * sine


def packed(real, imag):
    return halves(jnp.concatenate([real, imag], axis=1))


def outer_dft(dft_ref, first, second, sign):
    values = halves(jnp.concatenate([*first, *second], axis=1))
    by_cos = triple((dft_ref[0, 0], dft_ref[0, 1]), values)
    by_sin = triple((dft_ref[1, 0], dft_ref[1, 1]), values)
    found = []
    for low in (0, 2 * LANES):
        cos_real, cos_imag = by_cos[:, low : low + LANES], by_cos[:, low + LANES : low + 2 * LANES]
        sin_real, sin_imag = by_sin[:, low : low + LANES], by_sin[:, low + LANES : low + 2 * LANES]
        if sign > 0:
            found.append((cos_real - sin_imag, cos_imag + sin_real))
        else:
            found.append((cos_real + sin_imag, cos_imag - sin_real))
    return found


def disperse_kernel(in_ref, dft_ref, middle_ref, turn_ref, own_ref, out_ref, work):
    half = OUTER // 2
    middle = (middle_ref[0], middle_ref[1])
    for row in range(in_ref.shape[2]):
        real = in_ref[:, 0, row].reshape(OUTER, LANES)
        imag = in_ref[:, 1, row].reshape(OUTER, LANES)
        real, imag = turned(real, imag, own_ref[0, :OUTER], own_ref[1, :OUTER], -1)
        even = (real[:half] + real[half:], imag[:half] + imag[half:])
        odd = turned(real[:half] - real[half:], imag[:half] - imag[half:], *middle, -1)
        even, odd = outer_dft(dft_ref, even, odd, -1)
        real, imag = (jnp.concatenate([even[k], odd[k]], axis=0) for k in range(2))
        values = packed(*turned(real, imag, turn_ref[0], turn_ref[1], -1))
        both = triple(values, (dft_ref[2, 0], dft_ref[2, 1]))
        real, imag = turned(
            both[:, :LANES], both[:, LANES:], own_ref[2, :OUTER], own_ref[3, :OUTER], 1
        )
        both = triple(packed(real, imag), (dft_ref[3, 0], dft_ref[3, 1]))
        real, imag = turned(both[:, :LANES], both[:, LANES:], turn_ref[0], turn_ref[1], 1)
        even, odd = outer_dft(
            dft_ref, (real[:half], imag[:half]), (real[half:], imag[half:]), 1
        )
        odd = turned(*odd, *middle, 1)
        for part in range(2):
            work[part, :half] = even[part] + odd[part]
            work[part, half:OUTER] = even[part] - odd[part]
            work[part, OUTER : OUTER + REACH] = work[part, OUTER - REACH : OUTER]
            work[part, OUTER + REACH :] = work[part, :REACH]
        work[0], work[1] = turned(work[0], work[1], own_ref[0], own_ref[1], 1)
        for group in range(8):
            low, high = 64 * group, 64 * group + 64
            before = low - REACH if group else OUTER
            after = high if group < 7 else OUTER + REACH
            for part in range(2):
                out_ref[group, part, row, :64] = work[part, low:high]
                out_ref[group, part, row, 64 : 64 + REACH] = work[part, before : before + REACH]
                out_ref[group, part, row, 64 + REACH :] = work[part, after : after + REACH]


def disperse(values, own):
    outer, middle, turn, _ = tables()
    vmem = pl.BlockSpec(memory_space=VMEM)
    shape = values.shape[:3] + (64 + 2 * REACH, LANES)
    return pl.pallas_call(
        disperse_kernel,
        in_specs=[vmem] * 5,
        out_specs=vmem,
        out_shape=jax.ShapeDtypeStruct(shape, jnp.float32),
        scratch_shapes=[VMEM((2, OUTER + 2 * REACH, LANES), jnp.float32)],
        compiler_params=pltpu.CompilerParams(vmem_limit_bytes=32 * 1024 * 1024),
        name="disperse",
    )(values, np.concatenate([outer, inner_table()]), middle, turn, own)


def field_rows(part, row):
    low = (3 * part + row) * 64
    return slice(low, low + 64)


def unfold_kernel(in_ref, out_ref):
    rows = 8
    for step in range(in_ref.shape[3] // rows):
        at = slice(step * rows, step * rows + rows)
        squares = []
        for row in range(3):
            parts = [(in_ref[i, 0, row, at, :], in_ref[i, 1, row, at, :]) for i in range(COARSE)]
            results = radix_eight(parts, 1)
            if step < 8:
                for i, pair in enumerate(results):
                    for part in range(2):
                        low = field_rows(part, row).start + step * rows
                        out_ref[i, low : low + rows, :] = pair[part]
            else:
                squares.append([real * real + imag * imag for real, imag in results])
        if step == 8:
            for i in range(COARSE):
                out_ref[i, FIELD_ROWS : FIELD_ROWS + rows, :] = squares[0][i] + squares[1][i]
                out_ref[i, FIELD_ROWS + rows :, :] = squares[2][i]


def unfold(values):
    vmem = pl.BlockSpec(memory_space=VMEM)
    return pl.pallas_call(
        unfold_kernel,
        in_specs=[vmem],
        out_specs=vmem,
        out_shape=jax.ShapeDtypeStruct((COARSE, FIELD_ROWS + 4 * REACH, LANES), jnp.float32),
        compiler_params=pltpu.CompilerParams(vmem_limit_bytes=24 * 1024 * 1024),
        name="unfold",
    )(values)


def fields_of(held, chan):
    found = []
    for pol in range(2):
        group, row = (chan, pol) if chan < WHOLE else (2 * (chan - WHOLE) + pol, 2)
        found.append((held[group, field_rows(0, row), :], held[group, field_rows(1, row), :]))
    return found


def powers_around(held, chan):
    if chan < WHOLE:
        return held[chan, FIELD_ROWS : FIELD_ROWS + 2 * REACH, :]
    group = 2 * (chan - WHOLE)
    return held[group, FIELD_ROWS + 2 * REACH :, :] + held[group + 1, FIELD_ROWS + 2 * REACH :, :]


def sliding_sums(powers, around, table, extended):
    span = 64 + 2 * REACH
    extended[REACH : REACH + 64, :] = powers
    extended[:REACH, :] = around[:REACH]
    extended[64 + REACH : span, :] = around[REACH:]
    extended[span:, :] = jnp.zeros_like(around)
    both = jnp.concatenate([extended[:span, :], extended[1 : span + 1, :]], axis=1)
    upper, lower = halves(both)
    return dot(upper, table) + dot(lower, table)


def total(fields):
    return sum(real * real + imag * imag for real, imag in fields)


def trade(arrays):
    lanes = lax.broadcasted_iota(jnp.int32, arrays[0].shape, 1) // (LANES // GROUP)
    arrays = list(arrays)
    for bit in (1, 2, 4):
        width = bit * (LANES // GROUP)
        upper_half = (lanes & bit) != 0
        for low in range(GROUP):
            if low & bit:
                continue
            first, second = arrays[low], arrays[low | bit]
            arrays[low] = jnp.where(upper_half, pltpu.roll(second, width, 1), first)
            arrays[low | bit] = jnp.where(
                upper_half, second, pltpu.roll(first, LANES - width, 1)
            )
    return arrays


def slide_kernel(held, table_ref, out_ref, extended, sliding):
    local_chan = extended.shape[0]
    span = 64 + 2 * REACH
    rows = local_chan * TAKEN
    table = table_ref[...]
    for chan in range(local_chan):
        powers = total(fields_of(held, chan))
        around = powers_around(held, chan)
        sliding[span * chan : span * chan + span, :] = sliding_sums(
            powers, around, table, extended.at[chan]
        )
    for low in range(0, rows, 32):
        count = min(32, rows - low)
        parts = [
            sliding[pl.ds(low * GROUP + k, count, stride=GROUP), :] for k in range(GROUP)
        ]
        for group, part in enumerate(trade(parts)):
            out_ref[group, low : low + count, :] = part
    out_ref[:, rows:, :] = jnp.zeros_like(out_ref[:, rows:, :])


def slide_table():
    rows_idx = np.arange(2 * LANES)[:, None]
    cols_idx = np.arange(LANES)[None, :]
    return ((rows_idx >= cols_idx) & (rows_idx < cols_idx + LANES)).astype(ml_dtypes.bfloat16)


def slide(fields, groups, local_chan):
    vmem = pl.BlockSpec(memory_space=VMEM)
    return pl.pallas_call(
        slide_kernel,
        in_specs=[vmem, vmem],
        out_specs=vmem,
        out_shape=jax.ShapeDtypeStruct(
            (groups, -(-local_chan * TAKEN // 8) * 8, LANES), jnp.float32
        ),
        scratch_shapes=[
            VMEM((local_chan, 64 + 2 * REACH + 8, LANES), jnp.float32),
            VMEM((local_chan * (64 + 2 * REACH), LANES), jnp.float32),
        ],
        compiler_params=pltpu.CompilerParams(vmem_limit_bytes=24 * 1024 * 1024),
        name="slide",
    )(fields, slide_table())


def cross_kernel(starts_ref, lengths_ref, in_ref, out_ref, gathered, weights, uppers, lowers):
    channels = starts_ref.shape[0]
    devices = in_ref.shape[0]
    each = channels // devices
    shifts = 2 * HALO // LANES
    width = LANES // GROUP
    starts, lengths = starts_ref[...], lengths_ref[...]
    inverse = 1.0 / lengths.astype(jnp.float32)
    others = lax.broadcasted_iota(jnp.int32, starts.shape, 0) != lax.broadcasted_iota(
        jnp.int32, starts.shape, 1
    )
    nothing = jnp.zeros_like(inverse)
    for shift in range(shifts):
        offset = LANES * shift - HALO
        inside = (starts <= offset) & (offset + LANES <= starts + lengths)
        weights[:, shift * channels : (shift + 1) * channels] = jnp.where(
            inside & others, inverse, nothing
        )
    for step in range(TAKEN):
        for device in range(devices):
            gathered[step, device * each : (device + 1) * each, :] = in_ref[
                device, pl.ds(step, each, stride=TAKEN), :
            ]
    lanes = lax.broadcasted_iota(jnp.int32, (channels, LANES), 1)
    for shift in range(shifts):
        moved = [
            pltpu.roll(gathered[step], LANES - width * shift, 1) if shift else gathered[step]
            for step in range(TAKEN)
        ]
        at = slice(shift * channels, (shift + 1) * channels)
        for step in range(TAKEN - 1):
            values = moved[step]
            if shift:
                values = jnp.where(lanes < LANES - width * shift, values, moved[step + 1])
            uppers[step, at, :], lowers[step, at, :] = halves(values)
    pair_weights = halves(weights[...])
    for step in range(0, TAKEN - 1, 2):

        def pair(ref):
            return jnp.concatenate([ref[step], ref[step + 1]], axis=1)

        both = triple(pair_weights, (pair(uppers), pair(lowers)))
        out_ref[:, step, :] = both[:, :LANES]
        out_ref[:, step + 1, :] = both[:, LANES:]


def cross(starts, lengths, blocks):
    channels = starts.shape[0]
    depth = 2 * HALO // LANES * channels
    vmem = pl.BlockSpec(memory_space=VMEM)
    return pl.pallas_call(
        cross_kernel,
        in_specs=[vmem] * 3,
        out_specs=vmem,
        out_shape=jax.ShapeDtypeStruct((channels, TAKEN - 1, LANES), jnp.float32),
        scratch_shapes=[
            VMEM((TAKEN, channels, LANES), jnp.float32),
            VMEM((channels, depth), jnp.float32),
            VMEM((TAKEN - 1, depth, LANES), jnp.bfloat16),
            VMEM((TAKEN - 1, depth, LANES), jnp.bfloat16),
        ],
        compiler_params=pltpu.CompilerParams(vmem_limit_bytes=24 * 1024 * 1024),
        name="cross",
    )(starts, lengths, blocks)


def cosine_and_sine(angles):
    turns = jnp.floor(angles * np.float32(2.0 / np.pi) + 0.5)
    rest = ((angles - turns * 1.5703125) - turns * 4.837512969970703125e-4) - turns * np.float32(
        7.54978995489188216e-8
    )
    square = rest * rest
    sine = rest + rest * square * (
        -1.6666654611e-1 + square * (8.3321608736e-3 + square * -1.9515295891e-4)
    )
    cosine = (1.0 - 0.5 * square) + square * square * (
        4.166664568298827e-2 + square * (-1.388731625493765e-3 + square * 2.443315711809948e-5)
    )
    quadrant = turns.astype(jnp.int32) & 3
    swap = (quadrant & 1) == 1
    near, far = jnp.where(swap, sine, cosine), jnp.where(swap, cosine, sine)
    turned = (quadrant == 1) | (quadrant == 2)
    return jnp.where(turned, -near, near), jnp.where(quadrant >= 2, -far, far)


def tail_kernel(held, cross_ref, noise_ref, out_ref, cross_sum):
    rows = cross_ref.shape[1]
    for low in range(0, rows, 32):
        parts = [cross_ref[group, low : low + 32, :] for group in range(GROUP)]
        for k, part in enumerate(trade(parts)):
            cross_sum[pl.ds(low * GROUP + k, 32, stride=GROUP), :] = part
    for chan in range(out_ref.shape[1]):
        fields = fields_of(held, chan)
        others = cross_sum[64 * chan : 64 * chan + 64, :]
        cosine, sine = cosine_and_sine(GAMMA_SELF * total(fields) + GAMMA_CROSS * others)
        for pol, (real, imag) in enumerate(fields):
            at = pl.ds(pol, 64, stride=2)
            out_ref[0, chan, at, :] = cosine * real - sine * imag
            out_ref[1, chan, at, :] = cosine * imag + sine * real
        for part in range(2):
            out_ref[part, chan] = out_ref[part, chan] + noise_ref[part, chan].astype(jnp.float32)


def tail(fields, cross_sum, amp_noise):
    local_chan = cross_sum.shape[1] * GROUP // 64
    vmem = pl.BlockSpec(memory_space=VMEM)
    received = pl.pallas_call(
        tail_kernel,
        in_specs=[vmem] * 3,
        out_specs=vmem,
        out_shape=jax.ShapeDtypeStruct((2, local_chan, 128, LANES), jnp.float32),
        scratch_shapes=[VMEM((64 * local_chan, LANES), jnp.float32)],
        compiler_params=pltpu.CompilerParams(vmem_limit_bytes=24 * 1024 * 1024),
        name="tail",
    )(fields, cross_sum, interleaved(amp_noise))
    received = received.reshape(2, local_chan, 64, 2, LANES)
    return jnp.swapaxes(received, 2, 3).reshape(amp_noise.shape)


def exchange(values, axis):
    return lax.all_to_all(values, axis, 0, 0, tiled=True)


def per_device(launched, amp_noise, window_start, window_length):
    local_chan = launched.shape[1]
    groups = lax.axis_size("chan")
    own_tables = lax.dynamic_index_in_dim(
        jnp.asarray(tables()[3]), lax.axis_index("i"), 0, keepdims=False
    )
    values = exchange(head(launched), "j")
    values = exchange(fold(values), "i")
    values = exchange(disperse(values, own_tables), "i")
    fields = exchange(unfold(values), "j")
    blocks = exchange(slide(fields, groups, local_chan), "chan")
    cross_sum = cross(window_start, window_length, blocks)
    cross_sum = exchange(cross_sum.reshape(groups, -1, LANES), "chan")
    return tail(fields, cross_sum, amp_noise)


def solution(mesh):
    split = Mesh(mesh.devices.reshape(mesh.shape["chan"], COARSE, -1), ("chan", "j", "i"))
    fields = P(None, "chan", None, ("j", "i"))
    return jax.shard_map(
        per_device,
        mesh=split,
        in_specs=(fields, fields, P(), P()),
        out_specs=fields,
        check_vma=False,
    )
```

```python
import functools

import jax
import jax.numpy as jnp
import ml_dtypes
import numpy as np
from jax import lax
from jax.experimental import pallas as pl
from jax.experimental.pallas import tpu as pltpu
from jax.sharding import Mesh
from jax.sharding import PartitionSpec as P

HALO = 512
GAMMA_SELF = 0.1
GAMMA_CROSS = 0.05
SAMPLES = 524288
LANES = 128
COARSE = 8
FOLDED = SAMPLES // COARSE
OUTER = FOLDED // LANES
REACH = HALO // LANES
WHOLE = 8
GROUP = 8
TAKEN = 64 // GROUP + 1
FIELD_ROWS = 2 * 3 * 64
SMEM = pltpu.SMEM
VMEM = pltpu.VMEM


def split_np(matrix):
    upper = matrix.astype(ml_dtypes.bfloat16)
    lower = (matrix - upper.astype(np.float64)).astype(ml_dtypes.bfloat16)
    return np.stack([upper, lower])


def roots(numerators, period):
    angles = (numerators % period) * (2.0 * np.pi / period)
    return np.cos(angles), np.sin(angles)


@functools.cache
def inner_table():
    lane_ids = np.arange(LANES, dtype=np.int64)
    cosine, sine = roots(lane_ids[:, None] * lane_ids[None, :], LANES)
    forward = np.block([[cosine, -sine], [sine, cosine]])
    return np.stack([split_np(forward), split_np(forward.T)])


@functools.cache
def tables():
    outer_ids = np.arange(OUTER, dtype=np.int64)
    lane_ids = np.arange(LANES, dtype=np.int64)
    residues = np.arange(COARSE, dtype=np.int64)
    half = OUTER // 2
    half_ids = np.arange(half, dtype=np.int64)
    cosine, sine = roots(half_ids[:, None] * half_ids[None, :], half)
    outer = np.stack([split_np(cosine), split_np(sine)])
    middle = np.stack(roots(half_ids[:, None] + 0 * lane_ids[None, :], OUTER))
    order = np.concatenate([outer_ids[0::2], outer_ids[1::2]])
    turn = np.stack(roots(order[:, None] * lane_ids[None, :], FOLDED))
    around = np.concatenate([outer_ids, np.arange(-REACH, 0), OUTER + np.arange(REACH)])
    time_ids = LANES * around[:, None] + lane_ids[None, :]
    shift = np.stack(roots(residues[:, None, None] * time_ids[None], SAMPLES), axis=1)
    freq_ids = residues[:, None, None] + COARSE * (
        order[None, :, None] + OUTER * lane_ids[None, None, :]
    )
    signed_ids = np.where(freq_ids < SAMPLES // 2, freq_ids, freq_ids - SAMPLES)
    response = np.stack(roots(signed_ids * signed_ids, 4 * SAMPLES), axis=1) / SAMPLES
    response = np.pad(response, ((0, 0), (0, 0), (0, 2 * REACH), (0, 0)))
    by_residue = np.concatenate([shift, response], axis=1).astype(np.float32)
    return outer, middle.astype(np.float32), turn.astype(np.float32), by_residue


def radix_eight(parts, sign):
    half = np.float32(np.sqrt(0.5))

    def add(a, b):
        return a[0] + b[0], a[1] + b[1]

    def sub(a, b):
        return a[0] - b[0], a[1] - b[1]

    def quarter(a):
        return (-sign * a[1], sign * a[0])

    def eighth(a):
        return (half * (a[0] - sign * a[1]), half * (a[1] + sign * a[0]))

    def four(a, b, c, d):
        even_sum, even_diff = add(a, c), sub(a, c)
        odd_sum, odd_diff = add(b, d), quarter(sub(b, d))
        return (
            add(even_sum, odd_sum),
            add(even_diff, odd_diff),
            sub(even_sum, odd_sum),
            sub(even_diff, odd_diff),
        )

    even = four(*(add(parts[i], parts[i + 4]) for i in range(4)))
    diffs = [sub(parts[i], parts[i + 4]) for i in range(4)]
    odd = four(
        diffs[0], eighth(diffs[1]), quarter(diffs[2]), quarter(eighth(diffs[3]))
    )
    return [pair for both in zip(even, odd) for pair in both]


def rows_of(group):
    return ((group, 0), (group, 1), (WHOLE + group // 2, group % 2))


def head_kernel(in_ref, out_ref):
    for group in range(COARSE):
        for row, (chan, pol) in enumerate(rows_of(group)):
            for part in range(2):
                out_ref[group, part, row] = in_ref[part, chan, pl.ds(pol, 64, stride=2), :]


def head(launched):
    vmem = pl.BlockSpec(memory_space=VMEM)
    return pl.pallas_call(
        head_kernel,
        in_specs=[vmem],
        out_specs=vmem,
        out_shape=jax.ShapeDtypeStruct((COARSE, 2, 3, 64, LANES), jnp.float32),
        compiler_params=pltpu.CompilerParams(vmem_limit_bytes=24 * 1024 * 1024),
        name="head",
    )(interleaved(launched))


def interleaved(values):
    lead = values.shape[:-2]
    blocks = values.shape[-1] // LANES
    values = values.reshape(lead + (2, blocks, LANES))
    return jnp.swapaxes(values, -3, -2).reshape(lead + (2 * blocks, LANES))


def fold_kernel(in_ref, out_ref):
    rows = 8
    for row in range(in_ref.shape[2]):
        for step in range(in_ref.shape[3] // rows):
            at = slice(step * rows, step * rows + rows)
            parts = [(in_ref[i, 0, row, at, :], in_ref[i, 1, row, at, :]) for i in range(COARSE)]
            for i, pair in enumerate(radix_eight(parts, -1)):
                out_ref[i, 0, row, at, :] = pair[0]
                out_ref[i, 1, row, at, :] = pair[1]


def fold(values):
    vmem = pl.BlockSpec(memory_space=VMEM)
    return pl.pallas_call(
        fold_kernel,
        in_specs=[vmem],
        out_specs=vmem,
        out_shape=jax.ShapeDtypeStruct(values.shape, jnp.float32),
        compiler_params=pltpu.CompilerParams(vmem_limit_bytes=24 * 1024 * 1024),
        name="fold",
    )(values)


def halves(values):
    upper = values.astype(jnp.bfloat16)
    lower = (values - upper.astype(jnp.float32)).astype(jnp.bfloat16)
    return upper, lower


def dot(left, right):
    return jnp.dot(left, right, preferred_element_type=jnp.float32)


def triple(left, right):
    return dot(left[0], right[0]) + (dot(left[0], right[1]) + dot(left[1], right[0]))


def turned(real, imag, cosine, sine, sign):
    if sign > 0:
        return real * cosine - imag * sine, imag * cosine + real * sine
    return real * cosine + imag * sine, imag * cosine - real * sine


def packed(real, imag):
    return halves(jnp.concatenate([real, imag], axis=1))


def outer_dft(dft_ref, first, second, sign):
    values = halves(jnp.concatenate([*first, *second], axis=1))
    by_cos = triple((dft_ref[0, 0], dft_ref[0, 1]), values)
    by_sin = triple((dft_ref[1, 0], dft_ref[1, 1]), values)
    found = []
    for low in (0, 2 * LANES):
        cos_real, cos_imag = by_cos[:, low : low + LANES], by_cos[:, low + LANES : low + 2 * LANES]
        sin_real, sin_imag = by_sin[:, low : low + LANES], by_sin[:, low + LANES : low + 2 * LANES]
        if sign > 0:
            found.append((cos_real - sin_imag, cos_imag + sin_real))
        else:
            found.append((cos_real + sin_imag, cos_imag - sin_real))
    return found


def disperse_kernel(in_ref, dft_ref, middle_ref, turn_ref, own_ref, out_ref, work):
    half = OUTER // 2
    middle = (middle_ref[0], middle_ref[1])
    for row in range(in_ref.shape[2]):
        real = in_ref[:, 0, row].reshape(OUTER, LANES)
        imag = in_ref[:, 1, row].reshape(OUTER, LANES)
        real, imag = turned(real, imag, own_ref[0, :OUTER], own_ref[1, :OUTER], -1)
        even = (real[:half] + real[half:], imag[:half] + imag[half:])
        odd = turned(real[:half] - real[half:], imag[:half] - imag[half:], *middle, -1)
        even, odd = outer_dft(dft_ref, even, odd, -1)
        real, imag = (jnp.concatenate([even[k], odd[k]], axis=0) for k in range(2))
        values = packed(*turned(real, imag, turn_ref[0], turn_ref[1], -1))
        both = triple(values, (dft_ref[2, 0], dft_ref[2, 1]))
        real, imag = turned(
            both[:, :LANES], both[:, LANES:], own_ref[2, :OUTER], own_ref[3, :OUTER], 1
        )
        both = triple(packed(real, imag), (dft_ref[3, 0], dft_ref[3, 1]))
        real, imag = turned(both[:, :LANES], both[:, LANES:], turn_ref[0], turn_ref[1], 1)
        even, odd = outer_dft(
            dft_ref, (real[:half], imag[:half]), (real[half:], imag[half:]), 1
        )
        odd = turned(*odd, *middle, 1)
        for part in range(2):
            work[part, :half] = even[part] + odd[part]
            work[part, half:OUTER] = even[part] - odd[part]
            work[part, OUTER : OUTER + REACH] = work[part, OUTER - REACH : OUTER]
            work[part, OUTER + REACH :] = work[part, :REACH]
        work[0], work[1] = turned(work[0], work[1], own_ref[0], own_ref[1], 1)
        for group in range(8):
            low, high = 64 * group, 64 * group + 64
            before = low - REACH if group else OUTER
            after = high if group < 7 else OUTER + REACH
            for part in range(2):
                out_ref[group, part, row, :64] = work[part, low:high]
                out_ref[group, part, row, 64 : 64 + REACH] = work[part, before : before + REACH]
                out_ref[group, part, row, 64 + REACH :] = work[part, after : after + REACH]


def disperse(values, own):
    outer, middle, turn, _ = tables()
    vmem = pl.BlockSpec(memory_space=VMEM)
    shape = values.shape[:3] + (64 + 2 * REACH, LANES)
    return pl.pallas_call(
        disperse_kernel,
        in_specs=[vmem] * 5,
        out_specs=vmem,
        out_shape=jax.ShapeDtypeStruct(shape, jnp.float32),
        scratch_shapes=[VMEM((2, OUTER + 2 * REACH, LANES), jnp.float32)],
        compiler_params=pltpu.CompilerParams(vmem_limit_bytes=32 * 1024 * 1024),
        name="disperse",
    )(values, np.concatenate([outer, inner_table()]), middle, turn, own)


def field_rows(part, row):
    low = (3 * part + row) * 64
    return slice(low, low + 64)


def unfold_kernel(in_ref, out_ref):
    rows = 8
    for step in range(in_ref.shape[3] // rows):
        at = slice(step * rows, step * rows + rows)
        squares = []
        for row in range(3):
            parts = [(in_ref[i, 0, row, at, :], in_ref[i, 1, row, at, :]) for i in range(COARSE)]
            results = radix_eight(parts, 1)
            if step < 8:
                for i, pair in enumerate(results):
                    for part in range(2):
                        low = field_rows(part, row).start + step * rows
                        out_ref[i, low : low + rows, :] = pair[part]
            else:
                squares.append([real * real + imag * imag for real, imag in results])
        if step == 8:
            for i in range(COARSE):
                out_ref[i, FIELD_ROWS : FIELD_ROWS + rows, :] = squares[0][i] + squares[1][i]
                out_ref[i, FIELD_ROWS + rows :, :] = squares[2][i]


def unfold(values):
    vmem = pl.BlockSpec(memory_space=VMEM)
    return pl.pallas_call(
        unfold_kernel,
        in_specs=[vmem],
        out_specs=vmem,
        out_shape=jax.ShapeDtypeStruct((COARSE, FIELD_ROWS + 4 * REACH, LANES), jnp.float32),
        compiler_params=pltpu.CompilerParams(vmem_limit_bytes=24 * 1024 * 1024),
        name="unfold",
    )(values)


def fields_of(held, chan):
    found = []
    for pol in range(2):
        group, row = (chan, pol) if chan < WHOLE else (2 * (chan - WHOLE) + pol, 2)
        found.append((held[group, field_rows(0, row), :], held[group, field_rows(1, row), :]))
    return found


def powers_around(held, chan):
    if chan < WHOLE:
        return held[chan, FIELD_ROWS : FIELD_ROWS + 2 * REACH, :]
    group = 2 * (chan - WHOLE)
    return held[group, FIELD_ROWS + 2 * REACH :, :] + held[group + 1, FIELD_ROWS + 2 * REACH :, :]


def sliding_sums(powers, around, table, extended):
    span = 64 + 2 * REACH
    extended[REACH : REACH + 64, :] = powers
    extended[:REACH, :] = around[:REACH]
    extended[64 + REACH : span, :] = around[REACH:]
    extended[span:, :] = jnp.zeros_like(around)
    both = jnp.concatenate([extended[:span, :], extended[1 : span + 1, :]], axis=1)
    upper, lower = halves(both)
    return dot(upper, table) + dot(lower, table)


def total(fields):
    return sum(real * real + imag * imag for real, imag in fields)


def trade(arrays):
    lanes = lax.broadcasted_iota(jnp.int32, arrays[0].shape, 1) // (LANES // GROUP)
    arrays = list(arrays)
    for bit in (1, 2, 4):
        width = bit * (LANES // GROUP)
        upper_half = (lanes & bit) != 0
        for low in range(GROUP):
            if low & bit:
                continue
            first, second = arrays[low], arrays[low | bit]
            arrays[low] = jnp.where(upper_half, pltpu.roll(second, width, 1), first)
            arrays[low | bit] = jnp.where(
                upper_half, second, pltpu.roll(first, LANES - width, 1)
            )
    return arrays


def slide_kernel(held, table_ref, out_ref, extended, sliding):
    local_chan = extended.shape[0]
    span = 64 + 2 * REACH
    rows = local_chan * TAKEN
    table = table_ref[...]
    for chan in range(local_chan):
        powers = total(fields_of(held, chan))
        around = powers_around(held, chan)
        sliding[span * chan : span * chan + span, :] = sliding_sums(
            powers, around, table, extended.at[chan]
        )
    for low in range(0, rows, 32):
        count = min(32, rows - low)
        parts = [
            sliding[pl.ds(low * GROUP + k, count, stride=GROUP), :] for k in range(GROUP)
        ]
        for group, part in enumerate(trade(parts)):
            out_ref[group, low : low + count, :] = part
    out_ref[:, rows:, :] = jnp.zeros_like(out_ref[:, rows:, :])


def slide_table():
    rows_idx = np.arange(2 * LANES)[:, None]
    cols_idx = np.arange(LANES)[None, :]
    return ((rows_idx >= cols_idx) & (rows_idx < cols_idx + LANES)).astype(ml_dtypes.bfloat16)


def slide(fields, groups, local_chan):
    vmem = pl.BlockSpec(memory_space=VMEM)
    return pl.pallas_call(
        slide_kernel,
        in_specs=[vmem, vmem],
        out_specs=vmem,
        out_shape=jax.ShapeDtypeStruct(
            (groups, -(-local_chan * TAKEN // 8) * 8, LANES), jnp.float32
        ),
        scratch_shapes=[
            VMEM((local_chan, 64 + 2 * REACH + 8, LANES), jnp.float32),
            VMEM((local_chan * (64 + 2 * REACH), LANES), jnp.float32),
        ],
        compiler_params=pltpu.CompilerParams(vmem_limit_bytes=24 * 1024 * 1024),
        name="slide",
    )(fields, slide_table())


def cross_kernel(starts_ref, lengths_ref, in_ref, out_ref, gathered, weights, uppers, lowers):
    channels = starts_ref.shape[0]
    devices = in_ref.shape[0]
    each = channels // devices
    shifts = 2 * HALO // LANES
    width = LANES // GROUP
    starts, lengths = starts_ref[...], lengths_ref[...]
    inverse = 1.0 / lengths.astype(jnp.float32)
    others = lax.broadcasted_iota(jnp.int32, starts.shape, 0) != lax.broadcasted_iota(
        jnp.int32, starts.shape, 1
    )
    nothing = jnp.zeros_like(inverse)
    for shift in range(shifts):
        offset = LANES * shift - HALO
        inside = (starts <= offset) & (offset + LANES <= starts + lengths)
        weights[:, shift * channels : (shift + 1) * channels] = jnp.where(
            inside & others, inverse, nothing
        )
    for step in range(TAKEN):
        for device in range(devices):
            gathered[step, device * each : (device + 1) * each, :] = in_ref[
                device, pl.ds(step, each, stride=TAKEN), :
            ]
    lanes = lax.broadcasted_iota(jnp.int32, (channels, LANES), 1)
    for shift in range(shifts):
        moved = [
            pltpu.roll(gathered[step], LANES - width * shift, 1) if shift else gathered[step]
            for step in range(TAKEN)
        ]
        at = slice(shift * channels, (shift + 1) * channels)
        for step in range(TAKEN - 1):
            values = moved[step]
            if shift:
                values = jnp.where(lanes < LANES - width * shift, values, moved[step + 1])
            uppers[step, at, :], lowers[step, at, :] = halves(values)
    pair_weights = halves(weights[...])
    for step in range(0, TAKEN - 1, 2):

        def pair(ref):
            return jnp.concatenate([ref[step], ref[step + 1]], axis=1)

        both = triple(pair_weights, (pair(uppers), pair(lowers)))
        out_ref[:, step, :] = both[:, :LANES]
        out_ref[:, step + 1, :] = both[:, LANES:]


def cross(starts, lengths, blocks):
    channels = starts.shape[0]
    depth = 2 * HALO // LANES * channels
    vmem = pl.BlockSpec(memory_space=VMEM)
    return pl.pallas_call(
        cross_kernel,
        in_specs=[vmem] * 3,
        out_specs=vmem,
        out_shape=jax.ShapeDtypeStruct((channels, TAKEN - 1, LANES), jnp.float32),
        scratch_shapes=[
            VMEM((TAKEN, channels, LANES), jnp.float32),
            VMEM((channels, depth), jnp.float32),
            VMEM((TAKEN - 1, depth, LANES), jnp.bfloat16),
            VMEM((TAKEN - 1, depth, LANES), jnp.bfloat16),
        ],
        compiler_params=pltpu.CompilerParams(vmem_limit_bytes=24 * 1024 * 1024),
        name="cross",
    )(starts, lengths, blocks)


def cosine_and_sine(angles):
    turns = jnp.floor(angles * np.float32(2.0 / np.pi) + 0.5)
    rest = ((angles - turns * 1.5703125) - turns * 4.837512969970703125e-4) - turns * np.float32(
        7.54978995489188216e-8
    )
    square = rest * rest
    sine = rest + rest * square * (
        -1.6666654611e-1 + square * (8.3321608736e-3 + square * -1.9515295891e-4)
    )
    cosine = (1.0 - 0.5 * square) + square * square * (
        4.166664568298827e-2 + square * (-1.388731625493765e-3 + square * 2.443315711809948e-5)
    )
    quadrant = turns.astype(jnp.int32) & 3
    swap = (quadrant & 1) == 1
    near, far = jnp.where(swap, sine, cosine), jnp.where(swap, cosine, sine)
    turned = (quadrant == 1) | (quadrant == 2)
    return jnp.where(turned, -near, near), jnp.where(quadrant >= 2, -far, far)


def tail_kernel(held, cross_ref, noise_ref, out_ref, cross_sum, found, sent):
    rows = cross_ref.shape[1]
    for low in range(0, rows, 32):
        parts = [cross_ref[group, low : low + 32, :] for group in range(GROUP)]
        for k, part in enumerate(trade(parts)):
            cross_sum[pl.ds(low * GROUP + k, 32, stride=GROUP), :] = part
    part = 3

    def send(k):
        at = (slice(None), pl.ds(k * part, part))
        return pltpu.make_async_copy(found.at[at], out_ref.at[at], sent.at[k])

    for chan in range(out_ref.shape[1]):
        fields = fields_of(held, chan)
        others = cross_sum[64 * chan : 64 * chan + 64, :]
        cosine, sine = cosine_and_sine(GAMMA_SELF * total(fields) + GAMMA_CROSS * others)
        for pol, (real, imag) in enumerate(fields):
            at = pl.ds(pol, 64, stride=2)
            found[0, chan, at, :] = cosine * real - sine * imag
            found[1, chan, at, :] = cosine * imag + sine * real
        for side in range(2):
            found[side, chan] = found[side, chan] + noise_ref[side, chan].astype(jnp.float32)
        if chan % part == part - 1:
            send(chan // part).start()
    for k in range(out_ref.shape[1] // part):
        send(k).wait()


def tail(fields, cross_sum, amp_noise):
    local_chan = cross_sum.shape[1] * GROUP // 64
    vmem = pl.BlockSpec(memory_space=VMEM)
    received = pl.pallas_call(
        tail_kernel,
        in_specs=[vmem] * 3,
        out_specs=pl.BlockSpec(memory_space=pl.ANY),
        out_shape=jax.ShapeDtypeStruct((2, local_chan, 128, LANES), jnp.float32),
        scratch_shapes=[
            VMEM((64 * local_chan, LANES), jnp.float32),
            VMEM((2, local_chan, 128, LANES), jnp.float32),
            pltpu.SemaphoreType.DMA((local_chan // 3,)),
        ],
        compiler_params=pltpu.CompilerParams(vmem_limit_bytes=24 * 1024 * 1024),
        name="tail",
    )(fields, cross_sum, interleaved(amp_noise))
    received = received.reshape(2, local_chan, 64, 2, LANES)
    return jnp.swapaxes(received, 2, 3).reshape(amp_noise.shape)


def exchange(values, axis):
    return lax.all_to_all(values, axis, 0, 0, tiled=True)


def per_device(launched, amp_noise, window_start, window_length):
    local_chan = launched.shape[1]
    groups = lax.axis_size("chan")
    own_tables = lax.dynamic_index_in_dim(
        jnp.asarray(tables()[3]), lax.axis_index("i"), 0, keepdims=False
    )
    values, own_tables = lax.optimization_barrier((head(launched), own_tables))
    values = exchange(fold(exchange(values, "j")), "i")
    values = exchange(disperse(values, own_tables), "i")
    fields = exchange(unfold(values), "j")
    blocks = exchange(slide(fields, groups, local_chan), "chan")
    cross_sum = cross(window_start, window_length, blocks)
    cross_sum = exchange(cross_sum.reshape(groups, -1, LANES), "chan")
    return tail(fields, cross_sum, amp_noise)


def solution(mesh):
    split = Mesh(mesh.devices.reshape(mesh.shape["chan"], COARSE, -1), ("chan", "j", "i"))
    fields = P(None, "chan", None, ("j", "i"))
    return jax.shard_map(
        per_device,
        mesh=split,
        in_specs=(fields, fields, P(), P()),
        out_specs=fields,
        check_vma=False,
    )
```

```python
import functools

import jax
import jax.numpy as jnp
import ml_dtypes
import numpy as np
from jax import lax
from jax.experimental import pallas as pl
from jax.experimental.pallas import tpu as pltpu
from jax.sharding import Mesh
from jax.sharding import PartitionSpec as P

HALO = 512
GAMMA_SELF = 0.1
GAMMA_CROSS = 0.05
SAMPLES = 524288
LANES = 128
COARSE = 8
FOLDED = SAMPLES // COARSE
OUTER = FOLDED // LANES
REACH = HALO // LANES
WHOLE = 8
GROUP = 8
TAKEN = 64 // GROUP + 1
FIELD_ROWS = 2 * 3 * 64
SMEM = pltpu.SMEM
VMEM = pltpu.VMEM


def split_np(matrix):
    upper = matrix.astype(ml_dtypes.bfloat16)
    lower = (matrix - upper.astype(np.float64)).astype(ml_dtypes.bfloat16)
    return np.stack([upper, lower])


def roots(numerators, period):
    angles = (numerators % period) * (2.0 * np.pi / period)
    return np.cos(angles), np.sin(angles)


@functools.cache
def inner_table():
    lane_ids = np.arange(LANES, dtype=np.int64)
    cosine, sine = roots(lane_ids[:, None] * lane_ids[None, :], LANES)
    forward = np.block([[cosine, -sine], [sine, cosine]])
    return np.stack([split_np(forward), split_np(forward.T)])


@functools.cache
def tables():
    outer_ids = np.arange(OUTER, dtype=np.int64)
    lane_ids = np.arange(LANES, dtype=np.int64)
    residues = np.arange(COARSE, dtype=np.int64)
    half = OUTER // 2
    half_ids = np.arange(half, dtype=np.int64)
    cosine, sine = roots(half_ids[:, None] * half_ids[None, :], half)
    outer = np.stack([split_np(cosine), split_np(sine)])
    middle = np.stack(roots(half_ids[:, None] + 0 * lane_ids[None, :], OUTER))
    order = np.concatenate([outer_ids[0::2], outer_ids[1::2]])
    turn = np.stack(roots(order[:, None] * lane_ids[None, :], FOLDED))
    around = np.concatenate([outer_ids, np.arange(-REACH, 0), OUTER + np.arange(REACH)])
    time_ids = LANES * around[:, None] + lane_ids[None, :]
    shift = np.stack(roots(residues[:, None, None] * time_ids[None], SAMPLES), axis=1)
    freq_ids = residues[:, None, None] + COARSE * (
        order[None, :, None] + OUTER * lane_ids[None, None, :]
    )
    signed_ids = np.where(freq_ids < SAMPLES // 2, freq_ids, freq_ids - SAMPLES)
    response = np.stack(roots(signed_ids * signed_ids, 4 * SAMPLES), axis=1) / SAMPLES
    response = np.pad(response, ((0, 0), (0, 0), (0, 2 * REACH), (0, 0)))
    by_residue = np.concatenate([shift, response], axis=1).astype(np.float32)
    return outer, middle.astype(np.float32), turn.astype(np.float32), by_residue


def radix_eight(parts, sign):
    half = np.float32(np.sqrt(0.5))

    def add(a, b):
        return a[0] + b[0], a[1] + b[1]

    def sub(a, b):
        return a[0] - b[0], a[1] - b[1]

    def quarter(a):
        return (-sign * a[1], sign * a[0])

    def eighth(a):
        return (half * (a[0] - sign * a[1]), half * (a[1] + sign * a[0]))

    def four(a, b, c, d):
        even_sum, even_diff = add(a, c), sub(a, c)
        odd_sum, odd_diff = add(b, d), quarter(sub(b, d))
        return (
            add(even_sum, odd_sum),
            add(even_diff, odd_diff),
            sub(even_sum, odd_sum),
            sub(even_diff, odd_diff),
        )

    even = four(*(add(parts[i], parts[i + 4]) for i in range(4)))
    diffs = [sub(parts[i], parts[i + 4]) for i in range(4)]
    odd = four(
        diffs[0], eighth(diffs[1]), quarter(diffs[2]), quarter(eighth(diffs[3]))
    )
    return [pair for both in zip(even, odd) for pair in both]


def rows_of(group):
    return ((group, 0), (group, 1), (WHOLE + group // 2, group % 2))


def head_kernel(in_ref, tables_ref, out_ref):
    for group in range(COARSE):
        for row, (chan, pol) in enumerate(rows_of(group)):
            for part in range(2):
                out_ref[group, part, row] = in_ref[part, chan, pl.ds(pol, 64, stride=2), :]


def head(launched, own_tables):
    vmem = pl.BlockSpec(memory_space=VMEM)
    return pl.pallas_call(
        head_kernel,
        in_specs=[vmem, vmem],
        out_specs=vmem,
        out_shape=jax.ShapeDtypeStruct((COARSE, 2, 3, 64, LANES), jnp.float32),
        compiler_params=pltpu.CompilerParams(vmem_limit_bytes=24 * 1024 * 1024),
        name="head",
    )(interleaved(launched), own_tables)


def interleaved(values):
    lead = values.shape[:-2]
    blocks = values.shape[-1] // LANES
    values = values.reshape(lead + (2, blocks, LANES))
    return jnp.swapaxes(values, -3, -2).reshape(lead + (2 * blocks, LANES))


def fold_kernel(in_ref, out_ref):
    rows = 8
    for row in range(in_ref.shape[2]):
        for step in range(in_ref.shape[3] // rows):
            at = slice(step * rows, step * rows + rows)
            parts = [(in_ref[i, 0, row, at, :], in_ref[i, 1, row, at, :]) for i in range(COARSE)]
            for i, pair in enumerate(radix_eight(parts, -1)):
                out_ref[i, 0, row, at, :] = pair[0]
                out_ref[i, 1, row, at, :] = pair[1]


def fold(values):
    vmem = pl.BlockSpec(memory_space=VMEM)
    return pl.pallas_call(
        fold_kernel,
        in_specs=[vmem],
        out_specs=vmem,
        out_shape=jax.ShapeDtypeStruct(values.shape, jnp.float32),
        compiler_params=pltpu.CompilerParams(vmem_limit_bytes=24 * 1024 * 1024),
        name="fold",
    )(values)


def halves(values):
    upper = values.astype(jnp.bfloat16)
    lower = (values - upper.astype(jnp.float32)).astype(jnp.bfloat16)
    return upper, lower


def dot(left, right):
    return jnp.dot(left, right, preferred_element_type=jnp.float32)


def triple(left, right):
    return dot(left[0], right[0]) + (dot(left[0], right[1]) + dot(left[1], right[0]))


def turned(real, imag, cosine, sine, sign):
    if sign > 0:
        return real * cosine - imag * sine, imag * cosine + real * sine
    return real * cosine + imag * sine, imag * cosine - real * sine


def packed(real, imag):
    return halves(jnp.concatenate([real, imag], axis=1))


def outer_dft(dft_ref, first, second, sign):
    values = halves(jnp.concatenate([*first, *second], axis=1))
    by_cos = triple((dft_ref[0, 0], dft_ref[0, 1]), values)
    by_sin = triple((dft_ref[1, 0], dft_ref[1, 1]), values)
    found = []
    for low in (0, 2 * LANES):
        cos_real, cos_imag = by_cos[:, low : low + LANES], by_cos[:, low + LANES : low + 2 * LANES]
        sin_real, sin_imag = by_sin[:, low : low + LANES], by_sin[:, low + LANES : low + 2 * LANES]
        if sign > 0:
            found.append((cos_real - sin_imag, cos_imag + sin_real))
        else:
            found.append((cos_real + sin_imag, cos_imag - sin_real))
    return found


def disperse_kernel(in_ref, dft_ref, middle_ref, turn_ref, own_ref, out_ref, work):
    half = OUTER // 2
    middle = (middle_ref[0], middle_ref[1])
    for row in range(in_ref.shape[2]):
        real = in_ref[:, 0, row].reshape(OUTER, LANES)
        imag = in_ref[:, 1, row].reshape(OUTER, LANES)
        real, imag = turned(real, imag, own_ref[0, :OUTER], own_ref[1, :OUTER], -1)
        even = (real[:half] + real[half:], imag[:half] + imag[half:])
        odd = turned(real[:half] - real[half:], imag[:half] - imag[half:], *middle, -1)
        even, odd = outer_dft(dft_ref, even, odd, -1)
        real, imag = (jnp.concatenate([even[k], odd[k]], axis=0) for k in range(2))
        values = packed(*turned(real, imag, turn_ref[0], turn_ref[1], -1))
        both = triple(values, (dft_ref[2, 0], dft_ref[2, 1]))
        real, imag = turned(
            both[:, :LANES], both[:, LANES:], own_ref[2, :OUTER], own_ref[3, :OUTER], 1
        )
        both = triple(packed(real, imag), (dft_ref[3, 0], dft_ref[3, 1]))
        real, imag = turned(both[:, :LANES], both[:, LANES:], turn_ref[0], turn_ref[1], 1)
        even, odd = outer_dft(
            dft_ref, (real[:half], imag[:half]), (real[half:], imag[half:]), 1
        )
        odd = turned(*odd, *middle, 1)
        for part in range(2):
            work[part, :half] = even[part] + odd[part]
            work[part, half:OUTER] = even[part] - odd[part]
            work[part, OUTER : OUTER + REACH] = work[part, OUTER - REACH : OUTER]
            work[part, OUTER + REACH :] = work[part, :REACH]
        work[0], work[1] = turned(work[0], work[1], own_ref[0], own_ref[1], 1)
        for group in range(8):
            low, high = 64 * group, 64 * group + 64
            before = low - REACH if group else OUTER
            after = high if group < 7 else OUTER + REACH
            for part in range(2):
                out_ref[group, part, row, :64] = work[part, low:high]
                out_ref[group, part, row, 64 : 64 + REACH] = work[part, before : before + REACH]
                out_ref[group, part, row, 64 + REACH :] = work[part, after : after + REACH]


def disperse(values, own):
    outer, middle, turn, _ = tables()
    vmem = pl.BlockSpec(memory_space=VMEM)
    shape = values.shape[:3] + (64 + 2 * REACH, LANES)
    return pl.pallas_call(
        disperse_kernel,
        in_specs=[vmem] * 5,
        out_specs=vmem,
        out_shape=jax.ShapeDtypeStruct(shape, jnp.float32),
        scratch_shapes=[VMEM((2, OUTER + 2 * REACH, LANES), jnp.float32)],
        compiler_params=pltpu.CompilerParams(vmem_limit_bytes=32 * 1024 * 1024),
        name="disperse",
    )(values, np.concatenate([outer, inner_table()]), middle, turn, own)


def field_rows(part, row):
    low = (3 * part + row) * 64
    return slice(low, low + 64)


def unfold_kernel(in_ref, out_ref):
    rows = 8
    for step in range(in_ref.shape[3] // rows):
        at = slice(step * rows, step * rows + rows)
        squares = []
        for row in range(3):
            parts = [(in_ref[i, 0, row, at, :], in_ref[i, 1, row, at, :]) for i in range(COARSE)]
            results = radix_eight(parts, 1)
            if step < 8:
                for i, pair in enumerate(results):
                    for part in range(2):
                        low = field_rows(part, row).start + step * rows
                        out_ref[i, low : low + rows, :] = pair[part]
            else:
                squares.append([real * real + imag * imag for real, imag in results])
        if step == 8:
            for i in range(COARSE):
                out_ref[i, FIELD_ROWS : FIELD_ROWS + rows, :] = squares[0][i] + squares[1][i]
                out_ref[i, FIELD_ROWS + rows :, :] = squares[2][i]


def unfold(values):
    vmem = pl.BlockSpec(memory_space=VMEM)
    return pl.pallas_call(
        unfold_kernel,
        in_specs=[vmem],
        out_specs=vmem,
        out_shape=jax.ShapeDtypeStruct((COARSE, FIELD_ROWS + 4 * REACH, LANES), jnp.float32),
        compiler_params=pltpu.CompilerParams(vmem_limit_bytes=24 * 1024 * 1024),
        name="unfold",
    )(values)


def fields_of(held, chan):
    found = []
    for pol in range(2):
        group, row = (chan, pol) if chan < WHOLE else (2 * (chan - WHOLE) + pol, 2)
        found.append((held[group, field_rows(0, row), :], held[group, field_rows(1, row), :]))
    return found


def powers_around(held, chan):
    if chan < WHOLE:
        return held[chan, FIELD_ROWS : FIELD_ROWS + 2 * REACH, :]
    group = 2 * (chan - WHOLE)
    return held[group, FIELD_ROWS + 2 * REACH :, :] + held[group + 1, FIELD_ROWS + 2 * REACH :, :]


def sliding_sums(powers, around, table, extended):
    span = 64 + 2 * REACH
    extended[REACH : REACH + 64, :] = powers
    extended[:REACH, :] = around[:REACH]
    extended[64 + REACH : span, :] = around[REACH:]
    extended[span:, :] = jnp.zeros_like(around)
    both = jnp.concatenate([extended[:span, :], extended[1 : span + 1, :]], axis=1)
    upper, lower = halves(both)
    return dot(upper, table) + dot(lower, table)


def total(fields):
    return sum(real * real + imag * imag for real, imag in fields)


def trade(arrays):
    lanes = lax.broadcasted_iota(jnp.int32, arrays[0].shape, 1) // (LANES // GROUP)
    arrays = list(arrays)
    for bit in (1, 2, 4):
        width = bit * (LANES // GROUP)
        upper_half = (lanes & bit) != 0
        for low in range(GROUP):
            if low & bit:
                continue
            first, second = arrays[low], arrays[low | bit]
            arrays[low] = jnp.where(upper_half, pltpu.roll(second, width, 1), first)
            arrays[low | bit] = jnp.where(
                upper_half, second, pltpu.roll(first, LANES - width, 1)
            )
    return arrays


def slide_kernel(held, table_ref, out_ref, extended, sliding):
    local_chan = extended.shape[0]
    span = 64 + 2 * REACH
    rows = local_chan * TAKEN
    table = table_ref[...]
    for chan in range(local_chan):
        powers = total(fields_of(held, chan))
        around = powers_around(held, chan)
        sliding[span * chan : span * chan + span, :] = sliding_sums(
            powers, around, table, extended.at[chan]
        )
    for low in range(0, rows, 32):
        count = min(32, rows - low)
        parts = [
            sliding[pl.ds(low * GROUP + k, count, stride=GROUP), :] for k in range(GROUP)
        ]
        for group, part in enumerate(trade(parts)):
            out_ref[group, low : low + count, :] = part
    out_ref[:, rows:, :] = jnp.zeros_like(out_ref[:, rows:, :])


def slide_table():
    rows_idx = np.arange(2 * LANES)[:, None]
    cols_idx = np.arange(LANES)[None, :]
    return ((rows_idx >= cols_idx) & (rows_idx < cols_idx + LANES)).astype(ml_dtypes.bfloat16)


def slide(fields, groups, local_chan):
    vmem = pl.BlockSpec(memory_space=VMEM)
    return pl.pallas_call(
        slide_kernel,
        in_specs=[vmem, vmem],
        out_specs=vmem,
        out_shape=jax.ShapeDtypeStruct(
            (groups, -(-local_chan * TAKEN // 8) * 8, LANES), jnp.float32
        ),
        scratch_shapes=[
            VMEM((local_chan, 64 + 2 * REACH + 8, LANES), jnp.float32),
            VMEM((local_chan * (64 + 2 * REACH), LANES), jnp.float32),
        ],
        compiler_params=pltpu.CompilerParams(vmem_limit_bytes=24 * 1024 * 1024),
        name="slide",
    )(fields, slide_table())


def cross_kernel(starts_ref, lengths_ref, in_ref, out_ref, gathered, weights, uppers, lowers):
    channels = starts_ref.shape[0]
    devices = in_ref.shape[0]
    each = channels // devices
    shifts = 2 * HALO // LANES
    width = LANES // GROUP
    starts, lengths = starts_ref[...], lengths_ref[...]
    inverse = 1.0 / lengths.astype(jnp.float32)
    others = lax.broadcasted_iota(jnp.int32, starts.shape, 0) != lax.broadcasted_iota(
        jnp.int32, starts.shape, 1
    )
    nothing = jnp.zeros_like(inverse)
    for shift in range(shifts):
        offset = LANES * shift - HALO
        inside = (starts <= offset) & (offset + LANES <= starts + lengths)
        weights[:, shift * channels : (shift + 1) * channels] = jnp.where(
            inside & others, inverse, nothing
        )
    for step in range(TAKEN):
        for device in range(devices):
            gathered[step, device * each : (device + 1) * each, :] = in_ref[
                device, pl.ds(step, each, stride=TAKEN), :
            ]
    lanes = lax.broadcasted_iota(jnp.int32, (channels, LANES), 1)
    for shift in range(shifts):
        moved = [
            pltpu.roll(gathered[step], LANES - width * shift, 1) if shift else gathered[step]
            for step in range(TAKEN)
        ]
        at = slice(shift * channels, (shift + 1) * channels)
        for step in range(TAKEN - 1):
            values = moved[step]
            if shift:
                values = jnp.where(lanes < LANES - width * shift, values, moved[step + 1])
            uppers[step, at, :], lowers[step, at, :] = halves(values)
    pair_weights = halves(weights[...])
    for step in range(0, TAKEN - 1, 2):

        def pair(ref):
            return jnp.concatenate([ref[step], ref[step + 1]], axis=1)

        both = triple(pair_weights, (pair(uppers), pair(lowers)))
        out_ref[:, step, :] = both[:, :LANES]
        out_ref[:, step + 1, :] = both[:, LANES:]


def cross(starts, lengths, blocks):
    channels = starts.shape[0]
    depth = 2 * HALO // LANES * channels
    vmem = pl.BlockSpec(memory_space=VMEM)
    return pl.pallas_call(
        cross_kernel,
        in_specs=[vmem] * 3,
        out_specs=vmem,
        out_shape=jax.ShapeDtypeStruct((channels, TAKEN - 1, LANES), jnp.float32),
        scratch_shapes=[
            VMEM((TAKEN, channels, LANES), jnp.float32),
            VMEM((channels, depth), jnp.float32),
            VMEM((TAKEN - 1, depth, LANES), jnp.bfloat16),
            VMEM((TAKEN - 1, depth, LANES), jnp.bfloat16),
        ],
        compiler_params=pltpu.CompilerParams(vmem_limit_bytes=24 * 1024 * 1024),
        name="cross",
    )(starts, lengths, blocks)


def cosine_and_sine(angles):
    turns = jnp.floor(angles * np.float32(2.0 / np.pi) + 0.5)
    rest = ((angles - turns * 1.5703125) - turns * 4.837512969970703125e-4) - turns * np.float32(
        7.54978995489188216e-8
    )
    square = rest * rest
    sine = rest + rest * square * (
        -1.6666654611e-1 + square * (8.3321608736e-3 + square * -1.9515295891e-4)
    )
    cosine = (1.0 - 0.5 * square) + square * square * (
        4.166664568298827e-2 + square * (-1.388731625493765e-3 + square * 2.443315711809948e-5)
    )
    quadrant = turns.astype(jnp.int32) & 3
    swap = (quadrant & 1) == 1
    near, far = jnp.where(swap, sine, cosine), jnp.where(swap, cosine, sine)
    turned = (quadrant == 1) | (quadrant == 2)
    return jnp.where(turned, -near, near), jnp.where(quadrant >= 2, -far, far)


def tail_kernel(held, cross_ref, noise_ref, out_ref, cross_sum, found, sent):
    rows = cross_ref.shape[1]
    for low in range(0, rows, 32):
        parts = [cross_ref[group, low : low + 32, :] for group in range(GROUP)]
        for k, part in enumerate(trade(parts)):
            cross_sum[pl.ds(low * GROUP + k, 32, stride=GROUP), :] = part
    part = 3

    def send(k):
        at = (slice(None), pl.ds(k * part, part))
        return pltpu.make_async_copy(found.at[at], out_ref.at[at], sent.at[k])

    for chan in range(out_ref.shape[1]):
        fields = fields_of(held, chan)
        others = cross_sum[64 * chan : 64 * chan + 64, :]
        cosine, sine = cosine_and_sine(GAMMA_SELF * total(fields) + GAMMA_CROSS * others)
        for pol, (real, imag) in enumerate(fields):
            at = pl.ds(pol, 64, stride=2)
            found[0, chan, at, :] = cosine * real - sine * imag
            found[1, chan, at, :] = cosine * imag + sine * real
        for side in range(2):
            found[side, chan] = found[side, chan] + noise_ref[side, chan].astype(jnp.float32)
        if chan % part == part - 1:
            send(chan // part).start()
    for k in range(out_ref.shape[1] // part):
        send(k).wait()


def tail(fields, cross_sum, amp_noise):
    local_chan = cross_sum.shape[1] * GROUP // 64
    vmem = pl.BlockSpec(memory_space=VMEM)
    received = pl.pallas_call(
        tail_kernel,
        in_specs=[vmem] * 3,
        out_specs=pl.BlockSpec(memory_space=pl.ANY),
        out_shape=jax.ShapeDtypeStruct((2, local_chan, 128, LANES), jnp.float32),
        scratch_shapes=[
            VMEM((64 * local_chan, LANES), jnp.float32),
            VMEM((2, local_chan, 128, LANES), jnp.float32),
            pltpu.SemaphoreType.DMA((local_chan // 3,)),
        ],
        compiler_params=pltpu.CompilerParams(vmem_limit_bytes=24 * 1024 * 1024),
        name="tail",
    )(fields, cross_sum, interleaved(amp_noise))
    received = received.reshape(2, local_chan, 64, 2, LANES)
    return jnp.swapaxes(received, 2, 3).reshape(amp_noise.shape)


def exchange(values, axis):
    return lax.all_to_all(values, axis, 0, 0, tiled=True)


def per_device(launched, amp_noise, window_start, window_length):
    local_chan = launched.shape[1]
    groups = lax.axis_size("chan")
    own_tables = lax.dynamic_index_in_dim(
        jnp.asarray(tables()[3]), lax.axis_index("i"), 0, keepdims=False
    )
    values = exchange(head(launched, own_tables), "j")
    values = exchange(fold(values), "i")
    values = exchange(disperse(values, own_tables), "i")
    fields = exchange(unfold(values), "j")
    blocks = exchange(slide(fields, groups, local_chan), "chan")
    cross_sum = cross(window_start, window_length, blocks)
    cross_sum = exchange(cross_sum.reshape(groups, -1, LANES), "chan")
    return tail(fields, cross_sum, amp_noise)


def solution(mesh):
    split = Mesh(mesh.devices.reshape(mesh.shape["chan"], COARSE, -1), ("chan", "j", "i"))
    fields = P(None, "chan", None, ("j", "i"))
    return jax.shard_map(
        per_device,
        mesh=split,
        in_specs=(fields, fields, P(), P()),
        out_specs=fields,
        check_vma=False,
    )
```

```python
import functools

import jax
import jax.numpy as jnp
import ml_dtypes
import numpy as np
from jax import lax
from jax.experimental import pallas as pl
from jax.experimental.pallas import tpu as pltpu
from jax.sharding import Mesh
from jax.sharding import PartitionSpec as P

HALO = 512
GAMMA_SELF = 0.1
GAMMA_CROSS = 0.05
SAMPLES = 524288
LANES = 128
COARSE = 8
FOLDED = SAMPLES // COARSE
OUTER = FOLDED // LANES
REACH = HALO // LANES
WHOLE = 8
GROUP = 8
TAKEN = 64 // GROUP + 1
FIELD_ROWS = 2 * 3 * 64
SMEM = pltpu.SMEM
VMEM = pltpu.VMEM


def split_np(matrix):
    upper = matrix.astype(ml_dtypes.bfloat16)
    lower = (matrix - upper.astype(np.float64)).astype(ml_dtypes.bfloat16)
    return np.stack([upper, lower])


def roots(numerators, period):
    angles = (numerators % period) * (2.0 * np.pi / period)
    return np.cos(angles), np.sin(angles)


@functools.cache
def inner_table():
    lane_ids = np.arange(LANES, dtype=np.int64)
    cosine, sine = roots(lane_ids[:, None] * lane_ids[None, :], LANES)
    forward = np.block([[cosine, -sine], [sine, cosine]])
    return np.stack([split_np(forward), split_np(forward.T)])


@functools.cache
def tables():
    outer_ids = np.arange(OUTER, dtype=np.int64)
    lane_ids = np.arange(LANES, dtype=np.int64)
    residues = np.arange(COARSE, dtype=np.int64)
    half = OUTER // 2
    half_ids = np.arange(half, dtype=np.int64)
    cosine, sine = roots(half_ids[:, None] * half_ids[None, :], half)
    outer = np.stack([split_np(cosine), split_np(sine)])
    middle = np.stack(roots(half_ids[:, None] + 0 * lane_ids[None, :], OUTER))
    order = np.concatenate([outer_ids[0::2], outer_ids[1::2]])
    turn = np.stack(roots(order[:, None] * lane_ids[None, :], FOLDED))
    around = np.concatenate([outer_ids, np.arange(-REACH, 0), OUTER + np.arange(REACH)])
    time_ids = LANES * around[:, None] + lane_ids[None, :]
    shift = np.stack(roots(residues[:, None, None] * time_ids[None], SAMPLES), axis=1)
    freq_ids = residues[:, None, None] + COARSE * (
        order[None, :, None] + OUTER * lane_ids[None, None, :]
    )
    signed_ids = np.where(freq_ids < SAMPLES // 2, freq_ids, freq_ids - SAMPLES)
    response = np.stack(roots(signed_ids * signed_ids, 4 * SAMPLES), axis=1) / SAMPLES
    response = np.pad(response, ((0, 0), (0, 0), (0, 2 * REACH), (0, 0)))
    by_residue = np.concatenate([shift, response], axis=1).astype(np.float32)
    return outer, middle.astype(np.float32), turn.astype(np.float32), by_residue


def radix_eight(parts, sign):
    half = np.float32(np.sqrt(0.5))

    def add(a, b):
        return a[0] + b[0], a[1] + b[1]

    def sub(a, b):
        return a[0] - b[0], a[1] - b[1]

    def quarter(a):
        return (-sign * a[1], sign * a[0])

    def eighth(a):
        return (half * (a[0] - sign * a[1]), half * (a[1] + sign * a[0]))

    def four(a, b, c, d):
        even_sum, even_diff = add(a, c), sub(a, c)
        odd_sum, odd_diff = add(b, d), quarter(sub(b, d))
        return (
            add(even_sum, odd_sum),
            add(even_diff, odd_diff),
            sub(even_sum, odd_sum),
            sub(even_diff, odd_diff),
        )

    even = four(*(add(parts[i], parts[i + 4]) for i in range(4)))
    diffs = [sub(parts[i], parts[i + 4]) for i in range(4)]
    odd = four(
        diffs[0], eighth(diffs[1]), quarter(diffs[2]), quarter(eighth(diffs[3]))
    )
    return [pair for both in zip(even, odd) for pair in both]


def rows_of(group):
    return ((group, 0), (group, 1), (WHOLE + group // 2, group % 2))


def head_kernel(in_ref, tables_ref, out_ref):
    for group in range(COARSE):
        for row, (chan, pol) in enumerate(rows_of(group)):
            for part in range(2):
                out_ref[group, part, row] = in_ref[part, chan, pl.ds(pol, 64, stride=2), :]


def head(launched, own_tables):
    vmem = pl.BlockSpec(memory_space=VMEM)
    return pl.pallas_call(
        head_kernel,
        in_specs=[vmem, vmem],
        out_specs=vmem,
        out_shape=jax.ShapeDtypeStruct((COARSE, 2, 3, 64, LANES), jnp.float32),
        compiler_params=pltpu.CompilerParams(vmem_limit_bytes=24 * 1024 * 1024),
        name="head",
    )(interleaved(launched), own_tables)


def interleaved(values):
    lead = values.shape[:-2]
    blocks = values.shape[-1] // LANES
    values = values.reshape(lead + (2, blocks, LANES))
    return jnp.swapaxes(values, -3, -2).reshape(lead + (2 * blocks, LANES))


def fold_kernel(in_ref, out_ref):
    rows = 8
    for row in range(in_ref.shape[2]):
        for step in range(in_ref.shape[3] // rows):
            at = slice(step * rows, step * rows + rows)
            parts = [(in_ref[i, 0, row, at, :], in_ref[i, 1, row, at, :]) for i in range(COARSE)]
            for i, pair in enumerate(radix_eight(parts, -1)):
                out_ref[i, 0, row, at, :] = pair[0]
                out_ref[i, 1, row, at, :] = pair[1]


def fold(values):
    vmem = pl.BlockSpec(memory_space=VMEM)
    return pl.pallas_call(
        fold_kernel,
        in_specs=[vmem],
        out_specs=vmem,
        out_shape=jax.ShapeDtypeStruct(values.shape, jnp.float32),
        compiler_params=pltpu.CompilerParams(vmem_limit_bytes=24 * 1024 * 1024),
        name="fold",
    )(values)


def halves(values):
    upper = values.astype(jnp.bfloat16)
    lower = (values - upper.astype(jnp.float32)).astype(jnp.bfloat16)
    return upper, lower


def dot(left, right):
    return jnp.dot(left, right, preferred_element_type=jnp.float32)


def triple(left, right):
    return dot(left[0], right[0]) + (dot(left[0], right[1]) + dot(left[1], right[0]))


def turned(real, imag, cosine, sine, sign):
    if sign > 0:
        return real * cosine - imag * sine, imag * cosine + real * sine
    return real * cosine + imag * sine, imag * cosine - real * sine


def packed(real, imag):
    return halves(jnp.concatenate([real, imag], axis=1))


def outer_dft(dft_ref, first, second, sign):
    values = halves(jnp.concatenate([*first, *second], axis=1))
    by_cos = triple((dft_ref[0, 0], dft_ref[0, 1]), values)
    by_sin = triple((dft_ref[1, 0], dft_ref[1, 1]), values)
    found = []
    for low in (0, 2 * LANES):
        cos_real, cos_imag = by_cos[:, low : low + LANES], by_cos[:, low + LANES : low + 2 * LANES]
        sin_real, sin_imag = by_sin[:, low : low + LANES], by_sin[:, low + LANES : low + 2 * LANES]
        if sign > 0:
            found.append((cos_real - sin_imag, cos_imag + sin_real))
        else:
            found.append((cos_real + sin_imag, cos_imag - sin_real))
    return found


def disperse_kernel(in_ref, dft_ref, middle_ref, turn_ref, own_ref, out_ref, work):
    half = OUTER // 2
    middle = (middle_ref[0], middle_ref[1])
    for row in range(in_ref.shape[2]):
        real = in_ref[:, 0, row].reshape(OUTER, LANES)
        imag = in_ref[:, 1, row].reshape(OUTER, LANES)
        real, imag = turned(real, imag, own_ref[0, :OUTER], own_ref[1, :OUTER], -1)
        even = (real[:half] + real[half:], imag[:half] + imag[half:])
        odd = turned(real[:half] - real[half:], imag[:half] - imag[half:], *middle, -1)
        even, odd = outer_dft(dft_ref, even, odd, -1)
        real, imag = (jnp.concatenate([even[k], odd[k]], axis=0) for k in range(2))
        values = packed(*turned(real, imag, turn_ref[0], turn_ref[1], -1))
        both = triple(values, (dft_ref[2, 0], dft_ref[2, 1]))
        real, imag = turned(
            both[:, :LANES], both[:, LANES:], own_ref[2, :OUTER], own_ref[3, :OUTER], 1
        )
        both = triple(packed(real, imag), (dft_ref[3, 0], dft_ref[3, 1]))
        real, imag = turned(both[:, :LANES], both[:, LANES:], turn_ref[0], turn_ref[1], 1)
        even, odd = outer_dft(
            dft_ref, (real[:half], imag[:half]), (real[half:], imag[half:]), 1
        )
        odd = turned(*odd, *middle, 1)
        for part in range(2):
            work[part, :half] = even[part] + odd[part]
            work[part, half:OUTER] = even[part] - odd[part]
            work[part, OUTER : OUTER + REACH] = work[part, OUTER - REACH : OUTER]
            work[part, OUTER + REACH :] = work[part, :REACH]
        for group in range(8):
            low, high = 64 * group, 64 * group + 64
            before = low - REACH if group else OUTER
            after = high if group < 7 else OUTER + REACH
            for start, stop, to in (
                (low, high, 0),
                (before, before + REACH, 64),
                (after, after + REACH, 64 + REACH),
            ):
                fields = turned(
                    work[0, start:stop],
                    work[1, start:stop],
                    own_ref[0, start:stop],
                    own_ref[1, start:stop],
                    1,
                )
                for part in range(2):
                    out_ref[group, part, row, to : to + stop - start] = fields[part]


def disperse(values, own):
    outer, middle, turn, _ = tables()
    vmem = pl.BlockSpec(memory_space=VMEM)
    shape = values.shape[:3] + (64 + 2 * REACH, LANES)
    return pl.pallas_call(
        disperse_kernel,
        in_specs=[vmem] * 5,
        out_specs=vmem,
        out_shape=jax.ShapeDtypeStruct(shape, jnp.float32),
        scratch_shapes=[VMEM((2, OUTER + 2 * REACH, LANES), jnp.float32)],
        compiler_params=pltpu.CompilerParams(vmem_limit_bytes=32 * 1024 * 1024),
        name="disperse",
    )(values, np.concatenate([outer, inner_table()]), middle, turn, own)


def field_rows(part, row):
    low = (3 * part + row) * 64
    return slice(low, low + 64)


def unfold_kernel(in_ref, out_ref):
    rows = 8
    for step in range(in_ref.shape[3] // rows):
        at = slice(step * rows, step * rows + rows)
        squares = []
        for row in range(3):
            parts = [(in_ref[i, 0, row, at, :], in_ref[i, 1, row, at, :]) for i in range(COARSE)]
            results = radix_eight(parts, 1)
            if step < 8:
                for i, pair in enumerate(results):
                    for part in range(2):
                        low = field_rows(part, row).start + step * rows
                        out_ref[i, low : low + rows, :] = pair[part]
            else:
                squares.append([real * real + imag * imag for real, imag in results])
        if step == 8:
            for i in range(COARSE):
                out_ref[i, FIELD_ROWS : FIELD_ROWS + rows, :] = squares[0][i] + squares[1][i]
                out_ref[i, FIELD_ROWS + rows :, :] = squares[2][i]


def unfold(values):
    vmem = pl.BlockSpec(memory_space=VMEM)
    return pl.pallas_call(
        unfold_kernel,
        in_specs=[vmem],
        out_specs=vmem,
        out_shape=jax.ShapeDtypeStruct((COARSE, FIELD_ROWS + 4 * REACH, LANES), jnp.float32),
        compiler_params=pltpu.CompilerParams(vmem_limit_bytes=24 * 1024 * 1024),
        name="unfold",
    )(values)


def fields_of(held, chan):
    found = []
    for pol in range(2):
        group, row = (chan, pol) if chan < WHOLE else (2 * (chan - WHOLE) + pol, 2)
        found.append((held[group, field_rows(0, row), :], held[group, field_rows(1, row), :]))
    return found


def powers_around(held, chan):
    if chan < WHOLE:
        return held[chan, FIELD_ROWS : FIELD_ROWS + 2 * REACH, :]
    group = 2 * (chan - WHOLE)
    return held[group, FIELD_ROWS + 2 * REACH :, :] + held[group + 1, FIELD_ROWS + 2 * REACH :, :]


def sliding_sums(powers, around, table, extended):
    span = 64 + 2 * REACH
    extended[REACH : REACH + 64, :] = powers
    extended[:REACH, :] = around[:REACH]
    extended[64 + REACH : span, :] = around[REACH:]
    extended[span:, :] = jnp.zeros_like(around)
    both = jnp.concatenate([extended[:span, :], extended[1 : span + 1, :]], axis=1)
    upper, lower = halves(both)
    return dot(upper, table) + dot(lower, table)


def total(fields):
    return sum(real * real + imag * imag for real, imag in fields)


def trade(arrays):
    lanes = lax.broadcasted_iota(jnp.int32, arrays[0].shape, 1) // (LANES // GROUP)
    arrays = list(arrays)
    for bit in (1, 2, 4):
        width = bit * (LANES // GROUP)
        upper_half = (lanes & bit) != 0
        for low in range(GROUP):
            if low & bit:
                continue
            first, second = arrays[low], arrays[low | bit]
            arrays[low] = jnp.where(upper_half, pltpu.roll(second, width, 1), first)
            arrays[low | bit] = jnp.where(
                upper_half, second, pltpu.roll(first, LANES - width, 1)
            )
    return arrays


def slide_kernel(held, table_ref, out_ref, extended, sliding):
    local_chan = extended.shape[0]
    span = 64 + 2 * REACH
    rows = local_chan * TAKEN
    table = table_ref[...]
    for chan in range(local_chan):
        powers = total(fields_of(held, chan))
        around = powers_around(held, chan)
        sliding[span * chan : span * chan + span, :] = sliding_sums(
            powers, around, table, extended.at[chan]
        )
    for low in range(0, rows, 32):
        count = min(32, rows - low)
        parts = [
            sliding[pl.ds(low * GROUP + k, count, stride=GROUP), :] for k in range(GROUP)
        ]
        for group, part in enumerate(trade(parts)):
            out_ref[group, low : low + count, :] = part
    out_ref[:, rows:, :] = jnp.zeros_like(out_ref[:, rows:, :])


def slide_table():
    rows_idx = np.arange(2 * LANES)[:, None]
    cols_idx = np.arange(LANES)[None, :]
    return ((rows_idx >= cols_idx) & (rows_idx < cols_idx + LANES)).astype(ml_dtypes.bfloat16)


def slide(fields, groups, local_chan):
    vmem = pl.BlockSpec(memory_space=VMEM)
    return pl.pallas_call(
        slide_kernel,
        in_specs=[vmem, vmem],
        out_specs=vmem,
        out_shape=jax.ShapeDtypeStruct(
            (groups, -(-local_chan * TAKEN // 8) * 8, LANES), jnp.float32
        ),
        scratch_shapes=[
            VMEM((local_chan, 64 + 2 * REACH + 8, LANES), jnp.float32),
            VMEM((local_chan * (64 + 2 * REACH), LANES), jnp.float32),
        ],
        compiler_params=pltpu.CompilerParams(vmem_limit_bytes=24 * 1024 * 1024),
        name="slide",
    )(fields, slide_table())


def cross_kernel(starts_ref, lengths_ref, in_ref, out_ref, gathered, weights, uppers, lowers):
    channels = starts_ref.shape[0]
    devices = in_ref.shape[0]
    each = channels // devices
    shifts = 2 * HALO // LANES
    width = LANES // GROUP
    starts, lengths = starts_ref[...], lengths_ref[...]
    inverse = 1.0 / lengths.astype(jnp.float32)
    others = lax.broadcasted_iota(jnp.int32, starts.shape, 0) != lax.broadcasted_iota(
        jnp.int32, starts.shape, 1
    )
    nothing = jnp.zeros_like(inverse)
    for shift in range(shifts):
        offset = LANES * shift - HALO
        inside = (starts <= offset) & (offset + LANES <= starts + lengths)
        weights[:, shift * channels : (shift + 1) * channels] = jnp.where(
            inside & others, inverse, nothing
        )
    for step in range(TAKEN):
        for device in range(devices):
            gathered[step, device * each : (device + 1) * each, :] = in_ref[
                device, pl.ds(step, each, stride=TAKEN), :
            ]
    lanes = lax.broadcasted_iota(jnp.int32, (channels, LANES), 1)
    for shift in range(shifts):
        moved = [
            pltpu.roll(gathered[step], LANES - width * shift, 1) if shift else gathered[step]
            for step in range(TAKEN)
        ]
        at = slice(shift * channels, (shift + 1) * channels)
        for step in range(TAKEN - 1):
            values = moved[step]
            if shift:
                values = jnp.where(lanes < LANES - width * shift, values, moved[step + 1])
            uppers[step, at, :], lowers[step, at, :] = halves(values)
    pair_weights = halves(weights[...])
    for step in range(0, TAKEN - 1, 2):

        def pair(ref):
            return jnp.concatenate([ref[step], ref[step + 1]], axis=1)

        both = triple(pair_weights, (pair(uppers), pair(lowers)))
        out_ref[:, step, :] = both[:, :LANES]
        out_ref[:, step + 1, :] = both[:, LANES:]


def cross(starts, lengths, blocks):
    channels = starts.shape[0]
    depth = 2 * HALO // LANES * channels
    vmem = pl.BlockSpec(memory_space=VMEM)
    return pl.pallas_call(
        cross_kernel,
        in_specs=[vmem] * 3,
        out_specs=vmem,
        out_shape=jax.ShapeDtypeStruct((channels, TAKEN - 1, LANES), jnp.float32),
        scratch_shapes=[
            VMEM((TAKEN, channels, LANES), jnp.float32),
            VMEM((channels, depth), jnp.float32),
            VMEM((TAKEN - 1, depth, LANES), jnp.bfloat16),
            VMEM((TAKEN - 1, depth, LANES), jnp.bfloat16),
        ],
        compiler_params=pltpu.CompilerParams(vmem_limit_bytes=24 * 1024 * 1024),
        name="cross",
    )(starts, lengths, blocks)


def cosine_and_sine(angles):
    turns = jnp.floor(angles * np.float32(2.0 / np.pi) + 0.5)
    rest = ((angles - turns * 1.5703125) - turns * 4.837512969970703125e-4) - turns * np.float32(
        7.54978995489188216e-8
    )
    square = rest * rest
    sine = rest + rest * square * (
        -1.6666654611e-1 + square * (8.3321608736e-3 + square * -1.9515295891e-4)
    )
    cosine = (1.0 - 0.5 * square) + square * square * (
        4.166664568298827e-2 + square * (-1.388731625493765e-3 + square * 2.443315711809948e-5)
    )
    quadrant = turns.astype(jnp.int32) & 3
    swap = (quadrant & 1) == 1
    near, far = jnp.where(swap, sine, cosine), jnp.where(swap, cosine, sine)
    turned = (quadrant == 1) | (quadrant == 2)
    return jnp.where(turned, -near, near), jnp.where(quadrant >= 2, -far, far)


def tail_kernel(held, cross_ref, noise_ref, out_ref, cross_sum, found, sent):
    rows = cross_ref.shape[1]
    for low in range(0, rows, 32):
        parts = [cross_ref[group, low : low + 32, :] for group in range(GROUP)]
        for k, part in enumerate(trade(parts)):
            cross_sum[pl.ds(low * GROUP + k, 32, stride=GROUP), :] = part
    part = 3

    def send(k):
        at = (slice(None), pl.ds(k * part, part))
        return pltpu.make_async_copy(found.at[at], out_ref.at[at], sent.at[k])

    for chan in range(out_ref.shape[1]):
        fields = fields_of(held, chan)
        others = cross_sum[64 * chan : 64 * chan + 64, :]
        cosine, sine = cosine_and_sine(GAMMA_SELF * total(fields) + GAMMA_CROSS * others)
        for pol, (real, imag) in enumerate(fields):
            at = pl.ds(pol, 64, stride=2)
            found[0, chan, at, :] = cosine * real - sine * imag
            found[1, chan, at, :] = cosine * imag + sine * real
        for side in range(2):
            found[side, chan] = found[side, chan] + noise_ref[side, chan].astype(jnp.float32)
        if chan % part == part - 1:
            send(chan // part).start()
    for k in range(out_ref.shape[1] // part):
        send(k).wait()


def tail(fields, cross_sum, amp_noise):
    local_chan = cross_sum.shape[1] * GROUP // 64
    vmem = pl.BlockSpec(memory_space=VMEM)
    received = pl.pallas_call(
        tail_kernel,
        in_specs=[vmem] * 3,
        out_specs=pl.BlockSpec(memory_space=pl.ANY),
        out_shape=jax.ShapeDtypeStruct((2, local_chan, 128, LANES), jnp.float32),
        scratch_shapes=[
            VMEM((64 * local_chan, LANES), jnp.float32),
            VMEM((2, local_chan, 128, LANES), jnp.float32),
            pltpu.SemaphoreType.DMA((local_chan // 3,)),
        ],
        compiler_params=pltpu.CompilerParams(vmem_limit_bytes=24 * 1024 * 1024),
        name="tail",
    )(fields, cross_sum, interleaved(amp_noise))
    received = received.reshape(2, local_chan, 64, 2, LANES)
    return jnp.swapaxes(received, 2, 3).reshape(amp_noise.shape)


def exchange(values, axis):
    return lax.all_to_all(values, axis, 0, 0, tiled=True)


def per_device(launched, amp_noise, window_start, window_length):
    local_chan = launched.shape[1]
    groups = lax.axis_size("chan")
    own_tables = lax.dynamic_index_in_dim(
        jnp.asarray(tables()[3]), lax.axis_index("i"), 0, keepdims=False
    )
    values = exchange(head(launched, own_tables), "j")
    values = exchange(fold(values), "i")
    values = exchange(disperse(values, own_tables), "i")
    fields = exchange(unfold(values), "j")
    blocks = exchange(slide(fields, groups, local_chan), "chan")
    cross_sum = cross(window_start, window_length, blocks)
    cross_sum = exchange(cross_sum.reshape(groups, -1, LANES), "chan")
    return tail(fields, cross_sum, amp_noise)


def solution(mesh):
    split = Mesh(mesh.devices.reshape(mesh.shape["chan"], COARSE, -1), ("chan", "j", "i"))
    fields = P(None, "chan", None, ("j", "i"))
    return jax.shard_map(
        per_device,
        mesh=split,
        in_specs=(fields, fields, P(), P()),
        out_specs=fields,
        check_vma=False,
    )
```
